32 devices in a mesh: chan: 8 (over z, core), freq: 4 (over y, x).
Axes of the slice: x: 2, y: 2, z: 4, core: 2. Of those that a mesh axis runs over, the one named last changes fastest.
Arguments:
- strain: bfloat16 [512, 30720], P('chan', 'freq'), may hold values from -500 to 500
- quality: int32 [512], replicated, may hold values 0 or 1
- offset_reach: int32 [512], replicated, may hold values from 128 to 256, as said below
Outputs:
- stacked: float32 [8, 2, 3840, 256], P('chan', None, 'freq')
The draws below stay inside these ranges and needn't reach their ends.
Inputs may be any that keep to these rules, and one draw needn't show every extreme that they name: `offset_reach`: 256 is reached by some channel.
All inputs are finite; a program needn't handle non-finite values.
Results may differ from the reference program's by a relative error of at most 0.011.
Values may be sent and summed in bfloat16 or wider, within the bound.
No kernel may reach another device: no remote copies, remote signals or barrier semaphores. Data moves between devices by JAX's collectives and lax.ppermute only.
A program may use at most 64 MiB of HBM per device.

```python
import math
import jax
import jax.numpy as jnp
from jax import lax

CH_DEV = 64
BAND = 256
TBLK = 128
L1 = 60
TIME = 30720
CHANNELS = 512
N_FREQ = 4


def draw_strain(key, part):
    gain_key, stretch_key, fluct_key = jax.random.split(key, 3)
    channel_gain = jnp.exp(jax.random.uniform(gain_key, (CHANNELS, 1), jnp.float32, 0.0, math.log(10.0)))
    stretch_gain = jnp.exp(jax.random.uniform(stretch_key, (1, TIME // 64), jnp.float32, 0.0, math.log(10.0)))
    stretch_gain = jnp.repeat(stretch_gain, 64, axis=1)
    fluctuation = jax.random.truncated_normal(fluct_key, -5.0, 5.0, (CHANNELS, TIME), jnp.float32)
    return (channel_gain * stretch_gain * fluctuation).astype(jnp.bfloat16)


def draw_offset_reach(key, part):
    base_key, pick_key, spot_key = jax.random.split(jax.random.fold_in(key, 7), 3)
    reach_value = jax.random.randint(base_key, (CHANNELS,), BAND // 2, BAND + 1)
    widest = jax.random.randint(pick_key, (CHANNELS,), 0, 16) == 0
    spot_index = jax.random.randint(spot_key, (), 0, CHANNELS)
    widest = widest | (jnp.arange(CHANNELS) == spot_index)
    return jnp.where(widest, BAND, reach_value).astype(jnp.int32)


def touch_ends(array, rng, least, high):
    longest = array.shape.index(max(array.shape))
    spots = []
    for shift in (0, 1):
        where = [jax.random.randint(jax.random.fold_in(rng, axis), (), 0, length) for axis, length in enumerate(array.shape)]
        where[longest] = (where[longest] + shift) % array.shape[longest]
        spots.append(tuple(where))
    return array.at[spots[0]].set(least).at[spots[1]].set(high)


def setup_inputs(seed: int = 0) -> dict:
    keys = jax.random.split(jax.random.key(seed), 4)
    return {
        "strain": draw_strain(jax.random.fold_in(keys[3], 71), 0),
        "quality": touch_ends((jax.random.randint(keys[1], (CHANNELS,), 0, 8) < 7).astype(jnp.int32), jax.random.fold_in(keys[1], 1), 0, 1),
        "offset_reach": draw_offset_reach(jax.random.fold_in(keys[3], 71), 0),
    }


band_low = 0.004
band_high = 0.48
level_eps = 1e-05
item_batch = 4
row_block = 32
highest = lax.Precision.HIGHEST

def tap_values(offset, half_span):
    window = 0.5 + 0.5 * jnp.cos(jnp.pi * offset / (half_span + 1))
    response = 2.0 * band_high * jnp.sinc(2.0 * band_high * offset) - 2.0 * band_low * jnp.sinc(2.0 * band_low * offset)
    return jnp.where(jnp.abs(offset) <= half_span, window * response, 0.0)

def stencil_tables(half_span, boxed):
    row_index = jnp.arange(half_span)[:, None]
    col_index = jnp.arange(half_span)[None, :]
    tables = []
    for shift_q in (-1, 0, 1):
        offset = (col_index - row_index - half_span * shift_q).astype(jnp.float32)
        if boxed:
            entry_value = jnp.where(jnp.abs(offset) <= half_span, 1.0, 0.0)
        else:
            entry_value = tap_values(offset, half_span)
        tables.append(entry_value)
    return jnp.stack(tables).astype(jnp.bfloat16)

def apply_stencil(blocks, tables):
    wide = blocks.astype(jnp.float32)
    kernel = tables.astype(jnp.float32)
    total = jnp.einsum('cbr,rp->cbp', wide[:, :-2], kernel[0], precision=highest)
    total = total + jnp.einsum('cbr,rp->cbp', wide[:, 1:-1], kernel[1], precision=highest)
    total = total + jnp.einsum('cbr,rp->cbp', wide[:, 2:], kernel[2], precision=highest)
    return total

def whiten(padded, half_span):
    channel_count = padded.shape[0]
    blocks = padded.reshape(channel_count, -1, half_span)
    filtered = apply_stencil(blocks, stencil_tables(half_span, False))
    magnitude = jnp.abs(filtered).astype(jnp.bfloat16)
    level = apply_stencil(magnitude, stencil_tables(half_span, True)) / (2 * half_span + 1)
    whitened = filtered[:, 1:-1, :] / (level + level_eps)
    return whitened.astype(jnp.bfloat16)

def spectra(whitened):
    count_a = whitened.shape[-2]
    half_span = whitened.shape[-1]
    length = count_a * half_span
    a_index = jnp.arange(count_a, dtype=jnp.int32)
    b_index = jnp.arange(half_span, dtype=jnp.int32)
    k_index = jnp.arange(half_span // 2, dtype=jnp.int32)
    angle = (a_index[:, None] * a_index[None, :] % count_a).astype(jnp.float32) * (2.0 * math.pi / count_a)
    first = jnp.concatenate([jnp.cos(angle), -jnp.sin(angle)], axis=1).astype(jnp.bfloat16)
    section = jnp.einsum('...ab,ak->...kb', whitened.astype(jnp.float32), first.astype(jnp.float32), precision=highest)
    section_re = section[..., :count_a, :]
    section_im = section[..., count_a:, :]
    twist = (a_index[:, None] * b_index[None, :] % length).astype(jnp.float32) * (2.0 * math.pi / length)
    cos_twist = jnp.cos(twist)
    sin_twist = jnp.sin(twist)
    twisted_re = (section_re * cos_twist + section_im * sin_twist).astype(jnp.bfloat16)
    twisted_im = (section_im * cos_twist - section_re * sin_twist).astype(jnp.bfloat16)
    turn = (b_index[:, None] * k_index[None, :] % half_span).astype(jnp.float32) * (2.0 * math.pi / half_span)
    cos_turn = jnp.cos(turn)
    sin_turn = jnp.sin(turn)
    upper = jnp.stack([cos_turn, -sin_turn], axis=2).reshape(half_span, half_span).astype(jnp.bfloat16)
    lower = jnp.stack([sin_turn, cos_turn], axis=2).reshape(half_span, half_span).astype(jnp.bfloat16)
    result = jnp.einsum('...kb,bj->...kj', twisted_re.astype(jnp.float32), upper.astype(jnp.float32), precision=highest)
    result = result + jnp.einsum('...kb,bj->...kj', twisted_im.astype(jnp.float32), lower.astype(jnp.float32), precision=highest)
    return (result * (1.0 / math.sqrt(length))).astype(jnp.bfloat16)

def skew_rows(matrix, keep):
    leading = matrix.shape[:-2]
    height = matrix.shape[-2]
    width = matrix.shape[-1]
    flat = matrix.reshape(leading + (height * width,))
    flat = jnp.pad(flat, [(0, 0)] * len(leading) + [(0, height)])
    return flat.reshape(leading + (height, width + 1))[..., :keep]

def pair_weights(quality_ext, reach_own, band):
    channel_count = reach_own.shape[0]
    ext_len = quality_ext.shape[0]
    partner = skew_rows(jnp.broadcast_to(quality_ext[None, :], (channel_count, ext_len)), band)
    offsets = jnp.arange(band, dtype=jnp.int32)[None, :]
    inside = (offsets < reach_own[:, None]).astype(jnp.int32)
    weight = quality_ext[:channel_count, None] * partner * inside
    total = lax.optimization_barrier(jnp.sum(weight.astype(jnp.float32), axis=0))
    return (weight.astype(jnp.bfloat16), jnp.maximum(total, 1.0))

def cross_item(item, weight, band):
    seg_count, ext_len, twice_bins = item.shape
    bin_count = twice_bins // 2
    channel_count = weight.shape[0]
    right = item.reshape(seg_count, ext_len, bin_count, 2).transpose(2, 3, 0, 1).reshape(bin_count, 2 * seg_count, ext_len)
    own = right[:, :, :channel_count]
    swapped = jnp.concatenate([own[:, seg_count:], -own[:, :seg_count]], axis=1)
    left = jnp.stack([own, swapped], axis=1)
    block_count = channel_count // row_block
    left = left.reshape(bin_count, 2, 2 * seg_count, block_count, row_block)
    windows = jnp.stack([right[:, :, row_block * block_index:row_block * block_index + row_block + band] for block_index in range(block_count)], axis=2)
    product = jnp.einsum('kgqjr,kqjw->kgjrw', left.astype(jnp.float32), windows.astype(jnp.float32), precision=highest).astype(jnp.bfloat16)
    diagonal = skew_rows(product, band).reshape(bin_count, 2, channel_count, band)
    return jnp.einsum('kgio,io->kgo', diagonal.astype(jnp.float32), weight.astype(jnp.float32), precision=highest)

def cross_block(extended, weight, count, band):
    items = jnp.moveaxis(extended, 2, 0)
    summed = lax.map(lambda item: cross_item(item, weight, band), items, batch_size=item_batch)
    summed = summed.transpose(2, 1, 0, 3)
    return summed / count[None, None, None, :]

def reference(strain, quality, offset_reach):
    channel_total = strain.shape[0]
    block_total = channel_total // CH_DEV
    hop_count = (BAND - 2) // CH_DEV + 1

    def block_spectra(block_index):
        start = (block_index * CH_DEV).astype(jnp.int32)
        rows_block = lax.dynamic_slice_in_dim(strain, start, CH_DEV, 0)
        padded = jnp.pad(rows_block, ((0, 0), (2 * TBLK, 2 * TBLK)))
        whitened = whiten(padded, TBLK)
        segments = whitened.reshape(CH_DEV, N_FREQ, L1, TBLK)
        return spectra(segments)
    every = lax.map(block_spectra, jnp.arange(block_total, dtype=jnp.int32))
    every = every.transpose(2, 0, 1, 3, 4).reshape(N_FREQ, channel_total, L1, TBLK)
    every = jnp.pad(every, ((0, 0), (0, CH_DEV * hop_count), (0, 0), (0, 0)))
    quality_pad = jnp.concatenate([quality, jnp.zeros((CH_DEV * hop_count,), jnp.int32)])

    def block_stack(block_index):
        start = (block_index * CH_DEV).astype(jnp.int32)
        extended = lax.dynamic_slice_in_dim(every, start, CH_DEV * (hop_count + 1), 1)
        quality_ext = lax.dynamic_slice_in_dim(quality_pad, start, CH_DEV * (hop_count + 1), 0)
        reach_own = lax.dynamic_slice_in_dim(offset_reach, start, CH_DEV, 0)
        weight, count = pair_weights(quality_ext, reach_own, BAND)
        return cross_block(extended, weight, count, BAND)
    stacked = lax.map(block_stack, jnp.arange(block_total, dtype=jnp.int32))
    return stacked.reshape(block_total, 2, TBLK // 2 * L1, BAND)
```

```python
import functools
import math

import jax
import jax.numpy as jnp
import ml_dtypes
import numpy as np
from jax import lax
from jax.experimental import pallas as pl
from jax.experimental.pallas import tpu as pltpu
from jax.sharding import PartitionSpec as P

BAND = 256
TBLK = 128

band_low = 0.004
band_high = 0.48
level_eps = 1e-05
MIB = 1 << 20


def tap_values(offset, half_span):
    window = 0.5 + 0.5 * np.cos(np.pi * offset / (half_span + 1))
    response = 2.0 * band_high * np.sinc(2.0 * band_high * offset) - 2.0 * band_low * np.sinc(
        2.0 * band_low * offset
    )
    return np.where(np.abs(offset) <= half_span, window * response, 0.0)


def stencil_table(boxed):
    offset = np.arange(2 * TBLK)[None, :] + TBLK - np.arange(4 * TBLK)[:, None]
    if boxed:
        values = np.where(np.abs(offset) <= TBLK, 1.0, 0.0)
    else:
        values = tap_values(offset.astype(np.float64), TBLK)
    return values.astype(ml_dtypes.bfloat16)


def dft_tables(count_a, n_freq):
    pad_a = -(-count_a // 16) * 16
    length = count_a * TBLK
    index = np.arange(count_a)
    angle = (index[:, None] * index[None, :] % count_a) * (2.0 * np.pi / count_a)
    first = np.zeros((2, pad_a, pad_a))
    first[0, :count_a, :count_a] = np.cos(angle)
    first[1, :count_a, :count_a] = -np.sin(angle)
    first = first.reshape(2 * pad_a, pad_a).astype(ml_dtypes.bfloat16)
    twist = np.zeros((2, pad_a, TBLK), np.float32)
    turn = (index[:, None] * np.arange(TBLK)[None, :] % length) * (2.0 * np.pi / length)
    twist[0, :count_a] = np.cos(turn)
    twist[1, :count_a] = np.sin(turn)
    k2_count = TBLK // 2
    turn = (np.arange(k2_count)[:, None] * np.arange(TBLK)[None, :] % TBLK) * (2.0 * np.pi / TBLK)
    real = np.concatenate([np.cos(turn), np.sin(turn)], axis=1)
    imag = np.concatenate([-np.sin(turn), np.cos(turn)], axis=1)
    half = k2_count // n_freq // 2
    second = np.stack([real, imag]).reshape(2, n_freq, 2, half, 2 * TBLK)
    second = second.transpose(1, 2, 0, 3, 4).reshape(n_freq, 2, 2 * half, 2 * TBLK)
    return first, twist, second.astype(ml_dtypes.bfloat16)


def spectra_kernel(
    count_a,
    n_freq,
    meta,
    own,
    other,
    lo_own,
    lo_other,
    hi_own,
    hi_other,
    taps,
    box,
    first,
    twist,
    second,
    quality,
    *rest,
):
    outs = rest[:n_freq]
    padded, filtered, magnitude, whitened, tw_re, tw_im = rest[n_freq:]
    core, band = meta[0], meta[1]
    ch = own.shape[0]
    both = 2 * ch
    pad_a = first.shape[1]
    dot = functools.partial(jnp.dot, preferred_element_type=jnp.float32)

    for which, (lo, mid, hi) in enumerate(((lo_own, own, hi_own), (lo_other, other, hi_other))):
        base = core if which == 0 else 1 - core
        rows = pl.ds(pl.multiple_of(base * ch, ch), ch)
        for j in range(2):
            padded[j, rows, :] = lo[:, j * TBLK : (j + 1) * TBLK]
            padded[count_a + 2 + j, rows, :] = hi[:, j * TBLK : (j + 1) * TBLK]
        for j in range(count_a):
            padded[2 + j, rows, :] = mid[:, j * TBLK : (j + 1) * TBLK]

    def fir(i, carry):
        j = 2 * i
        window = jnp.concatenate([padded[j + n] for n in range(4)], axis=1)
        result = dot(window, taps[...])
        for n in range(2):
            part = result[:, n * TBLK : (n + 1) * TBLK]
            filtered[j + n] = part
            magnitude[j + n] = jnp.abs(part).astype(jnp.bfloat16)
        return carry

    lax.fori_loop(0, count_a // 2 + 1, fir, 0)

    def whiten(i, carry):
        j = 2 * i
        window = jnp.concatenate([magnitude[j + n] for n in range(4)], axis=1)
        level = dot(window, box[...]) / (2 * TBLK + 1)
        for n in range(2):
            part = filtered[j + n + 1] / (level[:, n * TBLK : (n + 1) * TBLK] + level_eps)
            rows = pl.ds(pl.multiple_of((j + n) * both, both), both)
            whitened[rows, :] = part
        return carry

    lax.fori_loop(0, count_a // 2, whiten, 0)
    whitened[count_a * both : pad_a * both, :] = jnp.zeros(
        ((pad_a - count_a) * both, TBLK), jnp.float32
    )

    def sections(i, carry):
        c = 2 * i
        pair = [
            whitened[pl.ds(c + n, pad_a, stride=both), :].astype(jnp.bfloat16) for n in range(2)
        ]
        section = dot(first[...], jnp.concatenate(pair, axis=1))
        for n in range(2):
            re = section[:pad_a, n * TBLK : (n + 1) * TBLK]
            im = section[pad_a:, n * TBLK : (n + 1) * TBLK]
            rows = pl.ds(pl.multiple_of((c + n) * pad_a, pad_a), pad_a)
            tw_re[rows, :] = re * twist[0] + im * twist[1]
            tw_im[rows, :] = im * twist[0] - re * twist[1]
        return carry

    lax.fori_loop(0, both // 2, sections, 0)

    rk = second.shape[2]
    group = max(1, 16 // rk)
    scale = quality[...] * (1.0 / math.sqrt(count_a * TBLK))
    turn = jnp.concatenate([second[band ^ d, core] for d in range(n_freq)], axis=0)

    def bins(i, carry):
        results = []
        for n in range(group):
            k1 = i * group + n
            re = tw_re[pl.ds(k1, both, stride=pad_a), :].astype(jnp.bfloat16)
            im = tw_im[pl.ds(k1, both, stride=pad_a), :].astype(jnp.bfloat16)
            result = lax.dot_general(
                turn,
                jnp.concatenate([re, im], axis=1),
                (((1,), (1,)), ((), ())),
                preferred_element_type=jnp.float32,
            )
            results.append(result * scale)
        rows = pl.ds(pl.multiple_of(i * group * rk, 16), group * rk)
        for d in range(n_freq):
            parts = [r[d * rk : (d + 1) * rk] for r in results]
            block = parts[0] if group == 1 else jnp.concatenate(parts, axis=0)
            outs[d][rows, :] = block.astype(jnp.bfloat16)
        return carry

    lax.fori_loop(0, count_a // group, bins, 0)


def spectra(meta, own, other, halos, quality, n_freq):
    ch, length = own.shape
    count_a = length // TBLK
    first, twist, second = dft_tables(count_a, n_freq)
    rk = second.shape[2]
    pad_a = first.shape[1]
    both = 2 * ch
    vmem = pl.BlockSpec(memory_space=pltpu.VMEM)
    return pl.pallas_call(
        functools.partial(spectra_kernel, count_a, n_freq),
        out_shape=[jax.ShapeDtypeStruct((count_a * rk, both), jnp.bfloat16)] * n_freq,
        in_specs=[pl.BlockSpec(memory_space=pltpu.SMEM)] + [vmem] * 12,
        out_specs=[vmem] * n_freq,
        scratch_shapes=[
            pltpu.VMEM((count_a + 4, both, TBLK), jnp.bfloat16),
            pltpu.VMEM((count_a + 2, both, TBLK), jnp.float32),
            pltpu.VMEM((count_a + 2, both, TBLK), jnp.bfloat16),
            pltpu.VMEM((pad_a * both, TBLK), jnp.float32),
            pltpu.VMEM((both * pad_a, TBLK), jnp.float32),
            pltpu.VMEM((both * pad_a, TBLK), jnp.float32),
        ],
        compiler_params=pltpu.CompilerParams(vmem_limit_bytes=48 * MIB),
        cost_estimate=pl.CostEstimate(
            flops=6 * 10**9, bytes_accessed=4 * 10**6, transcendentals=0
        ),
        name="spectra",
    )(
        meta,
        own,
        other,
        *halos,
        jnp.asarray(stencil_table(False)),
        jnp.asarray(stencil_table(True)),
        jnp.asarray(first),
        jnp.asarray(twist),
        jnp.asarray(second),
        quality,
    )


def cross_kernel(n_seg, rk, count_a, reach_own, reach_prev, *rest):
    turn_ref, pick_ref = rest[0], rest[1]
    own_refs = rest[2 : 2 + n_seg]
    prev_refs = rest[2 + n_seg : 2 + 2 * n_seg]
    next_refs = rest[2 + 2 * n_seg : 2 + 3 * n_seg]
    near_ref, far_ref, w_near, w_far, sums = rest[2 + 3 * n_seg :]
    step = pl.program_id(0)
    both = own_refs[0].shape[1]
    depth = turn_ref.shape[0]
    half = rk // 2
    nb = pick_ref.shape[0]
    nk1 = nb // half
    slabs = both // 8
    per_group = slabs // 2

    @pl.when(step == 0)
    def _():
        row = lax.broadcasted_iota(jnp.int32, (both, both), 0)
        col = lax.broadcasted_iota(jnp.int32, (both, both), 1)
        near = (col >= row) & (both + col - row < reach_own[...])
        far = (col < row) & (2 * both + col - row < reach_prev[...])
        w_near[...] = jnp.where(near, 1.0, 0.0)
        w_far[...] = jnp.where(far, 1.0, 0.0)

    def stacked(refs):
        return jnp.concatenate([r[...] for r in refs], axis=0)

    def left_rows(block):
        re = block.astype(jnp.float32).T.astype(jnp.bfloat16)
        im = jnp.dot(re, turn_ref[...], preferred_element_type=jnp.float32)
        re = re.astype(jnp.float32).reshape(slabs, 8, depth)
        im = im.reshape(slabs, 8, depth)
        return jnp.stack([re, im], axis=1).reshape(slabs, 16, depth).astype(jnp.bfloat16)

    own = stacked(own_refs)
    nxt = stacked(next_refs)
    right = jnp.concatenate([own, nxt], axis=1)
    left_own = left_rows(own)
    left_prev = left_rows(stacked(prev_refs))
    row = lax.broadcasted_iota(jnp.int32, (8, both), 0)
    col = lax.broadcasted_iota(jnp.int32, (8, both), 1)
    lead = col - row

    def bin_step(i, carry):
        pick = pick_ref[i][None]
        for g in range(2):
            here = slice(g * per_group, (g + 1) * per_group)
            rows = (left_own[here] * pick).reshape(per_group * 16, depth)
            near = jnp.dot(rows, right, preferred_element_type=jnp.float32)
            rows = (left_prev[here] * pick).reshape(per_group * 16, depth)
            far = jnp.dot(rows, nxt, preferred_element_type=jnp.float32)
            for p in range(2):
                acc = [None] * 3
                for n in range(per_group):
                    a = g * per_group + n
                    at = n * 16 + p * 8
                    local = near[at : at + 8, :both]
                    beyond = near[at : at + 8, both:]
                    distant = far[at : at + 8]
                    wn = w_near[a * 8 : a * 8 + 8, :]
                    wf = w_far[a * 8 : a * 8 + 8, :]
                    terms = (
                        jnp.where(lead >= 8 * a, local, beyond),
                        beyond * wn,
                        distant * wf,
                    )
                    shift = (both - 8 * a) % both
                    for r, term in enumerate(terms):
                        if shift:
                            term = pltpu.roll(term, shift, 1)
                        acc[r] = term if acc[r] is None else acc[r] + term
                for r in range(3):
                    sums[(r * 2 + g) * 2 + p, pl.ds(pl.multiple_of(i * 8, 8), 8), :] = acc[r]
        return carry

    lax.fori_loop(0, nb, bin_step, 0)

    def diagonal(r, g, p):
        total = None
        for b in range(8):
            part = sums[(r * 2 + g) * 2 + p, pl.ds(b, nb, stride=8), :]
            if b:
                part = pltpu.roll(part, both - b, 1)
            total = part if total is None else total + part
        return total

    far_parts = []
    for g in range(2):
        for p in range(2):
            for r in range(2):
                value = diagonal(r, g, p)
                for n in range(nk1):
                    near_ref[g, p, r, pl.ds(step * nk1 + n, half, stride=count_a), :] = value[
                        n * half : (n + 1) * half
                    ]
            far_parts.append(diagonal(2, g, p))
    far_ref[...] = jnp.concatenate(far_parts, axis=0).astype(jnp.bfloat16)


def cross(own, prev, nxt, reach_own, reach_prev, count_a, rk):
    n_seg = len(own)
    rows, both = own[0].shape
    half = rk // 2
    rb = 32 if n_seg <= 4 else 16
    depth = n_seg * rb
    nb = rb // 2
    steps = rows // rb
    lane = np.arange(depth)
    within = lane % rb
    part = within // half % 2
    bin_of = within // rk * half + within % half
    turn = np.zeros((depth, depth))
    turn[lane + np.where(part == 0, half, -half), lane] = np.where(part == 0, 1.0, -1.0)
    pick = (bin_of[None, None, :] == np.arange(nb)[:, None, None]).astype(np.float32)
    pick = np.broadcast_to(pick, (nb, 16, depth)).astype(ml_dtypes.bfloat16)
    whole = lambda shape: pl.BlockSpec(shape, lambda t: (0,) * len(shape))
    block = pl.BlockSpec((rb, both), lambda t: (t, 0))
    far_rows = 4 * nb
    return pl.pallas_call(
        functools.partial(cross_kernel, n_seg, rk, count_a),
        grid=(steps,),
        out_shape=[
            jax.ShapeDtypeStruct((2, 2, 2, rows // 2, both), jnp.float32),
            jax.ShapeDtypeStruct((steps * far_rows, both), jnp.bfloat16),
        ],
        in_specs=[
            whole((both, 1)),
            whole((both, 1)),
            whole(turn.shape),
            whole(pick.shape),
        ]
        + [block] * (3 * n_seg),
        out_specs=[
            whole((2, 2, 2, rows // 2, both)),
            pl.BlockSpec((far_rows, both), lambda t: (t, 0)),
        ],
        scratch_shapes=[
            pltpu.VMEM((both, both), jnp.float32),
            pltpu.VMEM((both, both), jnp.float32),
            pltpu.VMEM((12, nb * 8, both), jnp.float32),
        ],
        compiler_params=pltpu.CompilerParams(
            dimension_semantics=("arbitrary",), vmem_limit_bytes=48 * MIB
        ),
        cost_estimate=pl.CostEstimate(
            flops=30 * 10**9, bytes_accessed=6 * 10**6, transcendentals=0
        ),
        name="cross",
    )(
        reach_own,
        reach_prev,
        jnp.asarray(turn.astype(ml_dtypes.bfloat16)),
        jnp.asarray(pick),
        *own,
        *prev,
        *nxt,
    )


def finish_kernel(rk, count_a, nb, meta, mine, theirs, far_a, far_b, count, out_ref, total):
    core = meta[0]
    half = rk // 2
    nk1 = nb // half
    bins = mine.shape[2]
    inverse = 1.0 / count[...]
    both = far_a.shape[1]
    for which, (near, far) in enumerate(((mine, far_a), (theirs, far_b))):
        at = core if which == 0 else 1 - core
        rows = pl.ds(pl.multiple_of(at * bins, bins), bins)
        for p in range(2):
            total[p] = near[p, 1]

        def add(t, carry):
            for p in range(2):
                start = pl.multiple_of((t * 2 + p) * nb, nb)
                value = far[pl.ds(start, nb), :].astype(jnp.float32)
                for n in range(nk1):
                    place = pl.ds(t * nk1 + n, half, stride=count_a)
                    total[p, place, :] += value[n * half : (n + 1) * half]
            return carry

        lax.fori_loop(0, bins // nb, add, 0)
        for p in range(2):
            out_ref[p, rows, :both] = near[p, 0] * inverse[:, :both]
            out_ref[p, rows, both:] = total[p] * inverse[:, both:]


def finish(meta, mine, theirs, far_a, far_b, count, count_a, rk, nb):
    vmem = pl.BlockSpec(memory_space=pltpu.VMEM)
    bins = mine.shape[2]
    return pl.pallas_call(
        functools.partial(finish_kernel, rk, count_a, nb),
        out_shape=jax.ShapeDtypeStruct((2, 2 * bins, BAND), jnp.float32),
        in_specs=[pl.BlockSpec(memory_space=pltpu.SMEM)] + [vmem] * 5,
        out_specs=vmem,
        scratch_shapes=[pltpu.VMEM((2, bins, TBLK), jnp.float32)],
        compiler_params=pltpu.CompilerParams(vmem_limit_bytes=48 * MIB),
        name="finish",
    )(meta, mine, theirs, far_a, far_b, count)


def skew_rows(matrix, keep):
    height, width = matrix.shape
    flat = jnp.pad(matrix.reshape(height * width), (0, height))
    return flat.reshape(height, width + 1)[:, :keep]


def pair_count(quality_ext, reach_own, band):
    channel_count = reach_own.shape[0]
    ext_len = quality_ext.shape[0]
    partner = skew_rows(jnp.broadcast_to(quality_ext[None, :], (channel_count, ext_len)), band)
    offsets = jnp.arange(band, dtype=jnp.int32)[None, :]
    inside = (offsets < reach_own[:, None]).astype(jnp.int32)
    weight = quality_ext[:channel_count, None] * partner * inside
    return jnp.maximum(jnp.sum(weight.astype(jnp.float32), axis=0), 1.0)


def on_device(strain, quality, offset_reach):
    ch, length = strain.shape
    both = 2 * ch
    assert both == TBLK and BAND == 2 * both
    n_chan, n_freq = lax.axis_size("chan"), lax.axis_size("freq")
    count_a = length // TBLK
    rk = TBLK // 2 // n_freq
    me, band = lax.axis_index("chan"), lax.axis_index("freq")
    core, chip = me % 2, me // 2

    def moved(x, target):
        pairs = []
        for c in range(n_chan):
            for f in range(n_freq):
                to = target(c, f)
                if 0 <= to[0] < n_chan and 0 <= to[1] < n_freq:
                    pairs.append((c * n_freq + f, to[0] * n_freq + to[1]))
        return lax.ppermute(x, ("chan", "freq"), pairs)

    tail, head = strain[:, length - 2 * TBLK :], strain[:, : 2 * TBLK]
    other = moved(strain, lambda c, f: (c ^ 1, f))
    halos = [
        moved(tail, lambda c, f: (c, f + 1)),
        moved(tail, lambda c, f: (c ^ 1, f + 1)),
        moved(head, lambda c, f: (c, f - 1)),
        moved(head, lambda c, f: (c ^ 1, f - 1)),
    ]

    quality_pad = jnp.pad(quality, (0, BAND + both))
    reach_pad = jnp.pad(offset_reach, (both, 0))
    quality_both = lax.dynamic_slice_in_dim(quality_pad, chip * both, both, 0)
    reach_own = lax.dynamic_slice_in_dim(reach_pad, (chip + 1) * both, both, 0)[:, None]
    reach_prev = lax.dynamic_slice_in_dim(reach_pad, chip * both, both, 0)[:, None]
    quality_ext = lax.dynamic_slice_in_dim(quality_pad, me * ch, ch + BAND, 0)
    count = pair_count(quality_ext, lax.dynamic_slice_in_dim(offset_reach, me * ch, ch, 0), BAND)

    meta = jnp.stack([core, band]).astype(jnp.int32)
    parts = spectra(
        meta, strain, other, halos, quality_both.astype(jnp.float32)[None, :], n_freq
    )
    own = [parts[0]]
    for d in range(1, n_freq):
        own.append(moved(parts[d], lambda c, f, d=d: (c, f ^ d)))
    nxt = [moved(x, lambda c, f: (c - 2, f)) for x in own]
    prev = [moved(x, lambda c, f: (c + 2, f)) for x in own]
    near, far = cross(own, prev, nxt, reach_own, reach_prev, count_a, rk)
    nb = (32 if n_freq <= 4 else 16) // 2
    steps = far.shape[0] // (4 * nb)
    far = far.reshape(steps, 2, 2 * nb, both)
    pick = lambda x, axis, at: lax.dynamic_index_in_dim(x, at, axis, keepdims=False)
    theirs = moved(pick(near, 0, 1 - core), lambda c, f: (c ^ 1, f))
    far_a = moved(pick(far, 1, core).reshape(-1, both), lambda c, f: (c - 2, f))
    far_b = moved(pick(far, 1, 1 - core).reshape(-1, both), lambda c, f: ((c ^ 1) - 2, f))
    mine = pick(near, 0, core)
    out = finish(meta, mine, theirs, far_a, far_b, count[None, :], count_a, rk, nb)
    return out[None]


def solution(mesh):
    return jax.shard_map(
        on_device,
        mesh=mesh,
        in_specs=(P("chan", "freq"), P(), P()),
        out_specs=P("chan", None, "freq", None),
        check_vma=False,
    )
```

```python
import functools
import math

import jax
import jax.numpy as jnp
import ml_dtypes
import numpy as np
from jax import lax
from jax.experimental import pallas as pl
from jax.experimental.pallas import tpu as pltpu
from jax.sharding import PartitionSpec as P

BAND = 256
TBLK = 128

band_low = 0.004
band_high = 0.48
level_eps = 1e-05
MIB = 1 << 20


def tap_values(offset, half_span):
    window = 0.5 + 0.5 * np.cos(np.pi * offset / (half_span + 1))
    response = 2.0 * band_high * np.sinc(2.0 * band_high * offset) - 2.0 * band_low * np.sinc(
        2.0 * band_low * offset
    )
    return np.where(np.abs(offset) <= half_span, window * response, 0.0)


def stencil_table(boxed):
    offset = np.arange(2 * TBLK)[None, :] + TBLK - np.arange(4 * TBLK)[:, None]
    if boxed:
        values = np.where(np.abs(offset) <= TBLK, 1.0, 0.0)
    else:
        values = tap_values(offset.astype(np.float64), TBLK)
    return values.astype(ml_dtypes.bfloat16)


def dft_tables(count_a, n_freq):
    pad_a = -(-count_a // 16) * 16
    length = count_a * TBLK
    index = np.arange(count_a)
    angle = (index[:, None] * index[None, :] % count_a) * (2.0 * np.pi / count_a)
    first = np.zeros((2, pad_a, pad_a))
    first[0, :count_a, :count_a] = np.cos(angle)
    first[1, :count_a, :count_a] = -np.sin(angle)
    first = first.reshape(2 * pad_a, pad_a).astype(ml_dtypes.bfloat16)
    twist = np.zeros((2, pad_a, TBLK), np.float32)
    turn = (index[:, None] * np.arange(TBLK)[None, :] % length) * (2.0 * np.pi / length)
    twist[0, :count_a] = np.cos(turn)
    twist[1, :count_a] = np.sin(turn)
    k2_count = TBLK // 2
    turn = (np.arange(k2_count)[:, None] * np.arange(TBLK)[None, :] % TBLK) * (2.0 * np.pi / TBLK)
    real = np.concatenate([np.cos(turn), np.sin(turn)], axis=1)
    imag = np.concatenate([-np.sin(turn), np.cos(turn)], axis=1)
    half = k2_count // n_freq // 2
    second = np.stack([real, imag]).reshape(2, n_freq, 2, half, 2 * TBLK)
    second = second.transpose(1, 2, 0, 3, 4).reshape(n_freq, 2, 2 * half, 2 * TBLK)
    return first, twist, second.astype(ml_dtypes.bfloat16)


def block_bins(n_freq):
    return 16 if n_freq <= 4 else 8


def whole(shape):
    return pl.BlockSpec(shape, lambda t: (0,) * len(shape))


def spectra_kernel(
    count_a,
    n_freq,
    meta,
    own,
    other,
    lo_own,
    lo_other,
    hi_own,
    hi_other,
    taps,
    box,
    first,
    twist,
    second,
    quality,
    *rest,
):
    outs = rest[:n_freq]
    padded, filtered, magnitude, whitened, tw_re, tw_im = rest[n_freq:]
    core, band = meta[0], meta[1]
    ch = own.shape[0]
    both = 2 * ch
    pad_a = first.shape[1]
    dot = functools.partial(jnp.dot, preferred_element_type=jnp.float32)

    for which, (lo, mid, hi) in enumerate(((lo_own, own, hi_own), (lo_other, other, hi_other))):
        base = core if which == 0 else 1 - core
        rows = pl.ds(pl.multiple_of(base * ch, ch), ch)
        for j in range(2):
            padded[j, rows, :] = lo[:, j * TBLK : (j + 1) * TBLK]
            padded[count_a + 2 + j, rows, :] = hi[:, j * TBLK : (j + 1) * TBLK]
        for j in range(count_a):
            padded[2 + j, rows, :] = mid[:, j * TBLK : (j + 1) * TBLK]

    def fir(i, carry):
        j = 2 * i
        window = jnp.concatenate([padded[j + n] for n in range(4)], axis=1)
        result = dot(window, taps[...])
        for n in range(2):
            part = result[:, n * TBLK : (n + 1) * TBLK]
            filtered[j + n] = part
            magnitude[j + n] = jnp.abs(part).astype(jnp.bfloat16)
        return carry

    lax.fori_loop(0, count_a // 2 + 1, fir, 0, unroll=True)

    def whiten(i, carry):
        j = 2 * i
        window = jnp.concatenate([magnitude[j + n] for n in range(4)], axis=1)
        level = dot(window, box[...]) / (2 * TBLK + 1)
        for n in range(2):
            part = filtered[j + n + 1] / (level[:, n * TBLK : (n + 1) * TBLK] + level_eps)
            rows = pl.ds(pl.multiple_of((j + n) * both, both), both)
            whitened[rows, :] = part
        return carry

    lax.fori_loop(0, count_a // 2, whiten, 0, unroll=True)
    whitened[count_a * both : pad_a * both, :] = jnp.zeros(
        ((pad_a - count_a) * both, TBLK), jnp.float32
    )

    def sections(i, carry):
        c = 2 * i
        pair = [
            whitened[pl.ds(c + n, pad_a, stride=both), :].astype(jnp.bfloat16) for n in range(2)
        ]
        section = dot(first[...], jnp.concatenate(pair, axis=1))
        for n in range(2):
            re = section[:pad_a, n * TBLK : (n + 1) * TBLK]
            im = section[pad_a:, n * TBLK : (n + 1) * TBLK]
            rows = pl.ds(pl.multiple_of((c + n) * pad_a, pad_a), pad_a)
            tw_re[rows, :] = re * twist[0] + im * twist[1]
            tw_im[rows, :] = im * twist[0] - re * twist[1]
        return carry

    lax.fori_loop(0, both // 2, sections, 0, unroll=True)

    rk = second.shape[2]
    half = rk // 2
    group = block_bins(n_freq) // half
    scale = quality[...] * (1.0 / math.sqrt(count_a * TBLK))
    turn = jnp.concatenate([second[band ^ d, core] for d in range(n_freq)], axis=0)

    def bins(i, carry):
        results = []
        for n in range(group):
            k1 = i * group + n
            re = tw_re[pl.ds(k1, both, stride=pad_a), :].astype(jnp.bfloat16)
            im = tw_im[pl.ds(k1, both, stride=pad_a), :].astype(jnp.bfloat16)
            result = lax.dot_general(
                turn,
                jnp.concatenate([re, im], axis=1),
                (((1,), (1,)), ((), ())),
                preferred_element_type=jnp.float32,
            )
            results.append(result * scale)
        rows = pl.ds(pl.multiple_of(i * group * rk, 16), group * rk)
        for d in range(n_freq):
            starts = [d * rk + p * half for p in range(2)]
            block = jnp.concatenate([r[s : s + half] for s in starts for r in results], axis=0)
            outs[d][rows, :] = block.astype(jnp.bfloat16)
        return carry

    lax.fori_loop(0, count_a // group, bins, 0, unroll=True)


def spectra(meta, own, other, halos, quality, n_freq):
    ch, length = own.shape
    count_a = length // TBLK
    first, twist, second = dft_tables(count_a, n_freq)
    rk = second.shape[2]
    pad_a = first.shape[1]
    both = 2 * ch
    tables = (stencil_table(False), stencil_table(True), first, twist, second)
    operands = (own, other, *halos, *(jnp.asarray(t) for t in tables), quality)
    return pl.pallas_call(
        functools.partial(spectra_kernel, count_a, n_freq),
        grid=(1,),
        out_shape=[jax.ShapeDtypeStruct((count_a * rk, both), jnp.bfloat16)] * n_freq,
        in_specs=[pl.BlockSpec(memory_space=pltpu.SMEM)] + [whole(x.shape) for x in operands],
        out_specs=[whole((count_a * rk, both))] * n_freq,
        scratch_shapes=[
            pltpu.VMEM((count_a + 4, both, TBLK), jnp.bfloat16),
            pltpu.VMEM((count_a + 2, both, TBLK), jnp.float32),
            pltpu.VMEM((count_a + 2, both, TBLK), jnp.bfloat16),
            pltpu.VMEM((pad_a * both, TBLK), jnp.float32),
            pltpu.VMEM((both * pad_a, TBLK), jnp.float32),
            pltpu.VMEM((both * pad_a, TBLK), jnp.float32),
        ],
        compiler_params=pltpu.CompilerParams(vmem_limit_bytes=62 * MIB),
        cost_estimate=pl.CostEstimate(
            flops=6 * 10**9, bytes_accessed=4 * 10**6, transcendentals=0
        ),
        name="spectra",
    )(meta, *operands)


def cross_kernel(n_seg, half, count_a, reach_own, reach_prev, *rest):
    turn_ref, pick_ref, cut_ref = rest[:3]
    own_refs = rest[3 : 3 + n_seg]
    prev_refs = rest[3 + n_seg : 3 + 2 * n_seg]
    next_refs = rest[3 + 2 * n_seg : 3 + 3 * n_seg]
    near_ref, far_ref, w_near, w_far, edge, sum_one, sum_two, sum_far = rest[3 + 3 * n_seg :]
    step = pl.program_id(0)
    both = own_refs[0].shape[1]
    depth = turn_ref.shape[0]
    nb = pick_ref.shape[0]
    nk1 = nb // half
    slabs = both // 8
    rb = 2 * nb
    block = pl.ds(pl.multiple_of(step * rb, rb), rb)

    @pl.when(step == 0)
    def _():
        row = lax.broadcasted_iota(jnp.int32, (16, both), 0) % 8
        col = lax.broadcasted_iota(jnp.int32, (16, both), 1)
        offset = both + col - row
        for a in range(slabs):
            mine = reach_own[a * 8 : a * 8 + 8, :]
            lent = reach_prev[a * 8 : a * 8 + 8, :]
            mine = jnp.concatenate([mine, mine], axis=0)
            lent = jnp.concatenate([lent, lent], axis=0)
            inner = col < both - 8 * a
            w_near[a] = jnp.where(inner & ((col < row) | (offset < mine)), 1.0, 0.0)
            w_far[a] = jnp.where(~inner & (offset < lent), 1.0, 0.0)
        row = lax.broadcasted_iota(jnp.int32, (both, 2 * both), 0)
        col = lax.broadcasted_iota(jnp.int32, (both, 2 * both), 1)
        same = (row // (both // 2)) == (col // both)
        for d in range(1, 8):
            hit = same & (col % both == both - d) & (row % 8 >= d)
            hit = hit & (2 * both - d < reach_prev[...])
            edge[(d - 1) * both : d * both, :] = jnp.where(hit, 1.0, 0.0).astype(jnp.bfloat16)

    def stacked(refs):
        return jnp.concatenate([r[block, :] for r in refs], axis=0)

    def left_rows(block):
        re = block.astype(jnp.float32).T.astype(jnp.bfloat16)
        im = jnp.dot(re, turn_ref[...], preferred_element_type=jnp.float32)
        re = re.astype(jnp.float32).reshape(slabs, 8, depth)
        im = im.reshape(slabs, 8, depth)
        return jnp.stack([re, im], axis=1).reshape(slabs, 16, depth).astype(jnp.bfloat16)

    own = stacked(own_refs)
    nxt = stacked(next_refs)
    prev = stacked(prev_refs)
    left = jnp.concatenate([left_rows(own), left_rows(prev)], axis=2)
    pick = pick_ref[...]

    zero = jnp.zeros_like(own)
    for a in range(slabs):
        g, first = divmod(a, slabs // 2)
        if a == 0:
            right = jnp.concatenate(
                [jnp.concatenate([own, nxt], axis=1), jnp.concatenate([zero, zero], axis=1)],
                axis=0,
            )
        else:
            moved_own = pltpu.roll(own, both - 8 * a, 1).reshape(depth // 16, 16, both)
            moved_next = pltpu.roll(nxt, both - 8 * a, 1).reshape(depth // 16, 16, both)
            cut = cut_ref[a][None]
            inner = moved_next * cut
            outer = moved_next - inner
            local = (moved_own * cut + outer).reshape(depth, both)
            inner = inner.reshape(depth, both)
            outer = outer.reshape(depth, both)
            right = jnp.concatenate(
                [
                    jnp.concatenate([local, inner], axis=1),
                    jnp.concatenate([zero, outer], axis=1),
                ],
                axis=0,
            )
        rows = (left[a][None] * pick).reshape(nb * 16, 2 * depth)
        result = jnp.dot(rows, right, preferred_element_type=jnp.float32)
        one = result[:, :both]
        two = result[:, both:].reshape(nb, 16, both)
        near = (two * w_near[a][None]).reshape(nb * 16, both)
        far = (two * w_far[a][None]).reshape(nb * 16, both)
        if first == 0:
            sum_one[g], sum_two[g], sum_far[g] = one, near, far
        else:
            sum_one[g] += one
            sum_two[g] += near
            sum_far[g] += far

    def split(ref):
        x = ref[block, :].astype(jnp.float32)
        return x[:nb], x[nb:]

    lefts = [split(r) for r in prev_refs]
    rights = [split(r) for r in next_refs]
    pieces = []
    for d in range(1, 8):
        re = im = None
        for (xr, xi), (yr, yi) in zip(lefts, rights):
            yr, yi = pltpu.roll(yr, d, 1), pltpu.roll(yi, d, 1)
            r, i = xr * yr + xi * yi, xi * yr - xr * yi
            re, im = (r, i) if re is None else (re + r, im + i)
        pieces.append(jnp.concatenate([re, im], axis=0).astype(jnp.bfloat16))
    margin = jnp.dot(
        jnp.concatenate(pieces, axis=1), edge[...], preferred_element_type=jnp.float32
    )

    lane = lax.broadcasted_iota(jnp.int32, (nb, both), 1)
    far_parts = []
    for g in range(2):
        for p in range(2):
            low = high = far = None
            for b in range(8):
                rows = pl.ds(p * 8 + b, nb, stride=16)
                one, two, three = sum_one[g, rows, :], sum_two[g, rows, :], sum_far[g, rows, :]
                if b == 0:
                    low, high, far = one, two, three
                    continue
                low += pltpu.roll(jnp.where(lane >= b, one, two), both - b, 1)
                high += pltpu.roll(jnp.where(lane >= b, two, 0.0), both - b, 1)
                far += pltpu.roll(three, both - b, 1)
            for r, value in enumerate((low, high)):
                for n in range(nk1):
                    near_ref[g, p, r, pl.ds(step * nk1 + n, half, stride=count_a), :] = value[
                        n * half : (n + 1) * half
                    ]
            far_parts.append(far + margin[p * nb : (p + 1) * nb, g * both : (g + 1) * both])
    far_ref[...] = jnp.concatenate(far_parts, axis=0).astype(jnp.bfloat16)


def cross(own, prev, nxt, reach_own, reach_prev, count_a, rk):
    n_seg = len(own)
    rows, both = own[0].shape
    half = rk // 2
    nb = block_bins(n_seg)
    rb = 2 * nb
    depth = n_seg * rb
    steps = rows // rb
    slabs = both // 8
    lane = np.arange(depth)
    part = lane % rb // nb
    turn = np.zeros((depth, depth))
    turn[lane + np.where(part == 0, nb, -nb), lane] = np.where(part == 0, 1.0, -1.0)
    lane = np.arange(2 * depth)
    pick = (lane % nb == np.arange(nb)[:, None, None]).astype(np.float32)
    pick = np.broadcast_to(pick, (nb, 16, 2 * depth))
    cut = np.arange(both) < both - 8 * np.arange(slabs)[:, None, None]
    cut = np.broadcast_to(cut, (slabs, 16, both))
    tables = [jnp.asarray(x.astype(ml_dtypes.bfloat16)) for x in (turn, pick, cut)]
    operands = (reach_own, reach_prev, *tables, *own, *prev, *nxt)
    far_rows = 4 * nb
    return pl.pallas_call(
        functools.partial(cross_kernel, n_seg, half, count_a),
        grid=(steps,),
        out_shape=[
            jax.ShapeDtypeStruct((2, 2, 2, rows // 2, both), jnp.float32),
            jax.ShapeDtypeStruct((steps * far_rows, both), jnp.bfloat16),
        ],
        in_specs=[whole(x.shape) for x in operands],
        out_specs=[
            whole((2, 2, 2, rows // 2, both)),
            pl.BlockSpec((far_rows, both), lambda t: (t, 0)),
        ],
        scratch_shapes=[
            pltpu.VMEM((slabs, 16, both), jnp.float32),
            pltpu.VMEM((slabs, 16, both), jnp.float32),
            pltpu.VMEM((7 * both, 2 * both), jnp.bfloat16),
            pltpu.VMEM((2, nb * 16, both), jnp.float32),
            pltpu.VMEM((2, nb * 16, both), jnp.float32),
            pltpu.VMEM((2, nb * 16, both), jnp.float32),
        ],
        compiler_params=pltpu.CompilerParams(
            dimension_semantics=("arbitrary",), vmem_limit_bytes=62 * MIB
        ),
        cost_estimate=pl.CostEstimate(
            flops=30 * 10**9, bytes_accessed=6 * 10**6, transcendentals=0
        ),
        name="cross",
    )(*operands)


def finish_kernel(rk, count_a, nb, meta, mine, theirs, far_a, far_b, count, out_ref, total):
    core = meta[0]
    half = rk // 2
    nk1 = nb // half
    bins = mine.shape[2]
    inverse = 1.0 / count[...]
    both = far_a.shape[1]
    for which, (near, far) in enumerate(((mine, far_a), (theirs, far_b))):
        at = core if which == 0 else 1 - core
        rows = pl.ds(pl.multiple_of(at * bins, bins), bins)
        for p in range(2):
            total[p] = near[p, 1]

        def add(t, carry):
            for p in range(2):
                start = pl.multiple_of((t * 2 + p) * nb, nb)
                value = far[pl.ds(start, nb), :].astype(jnp.float32)
                for n in range(nk1):
                    place = pl.ds(t * nk1 + n, half, stride=count_a)
                    total[p, place, :] += value[n * half : (n + 1) * half]
            return carry

        lax.fori_loop(0, bins // nb, add, 0, unroll=True)
        for p in range(2):
            out_ref[p, rows, :both] = near[p, 0] * inverse[:, :both]
            out_ref[p, rows, both:] = total[p] * inverse[:, both:]


def finish(meta, mine, theirs, far_a, far_b, count, count_a, rk, nb):
    bins = mine.shape[2]
    operands = (mine, theirs, far_a, far_b, count)
    return pl.pallas_call(
        functools.partial(finish_kernel, rk, count_a, nb),
        grid=(1,),
        out_shape=jax.ShapeDtypeStruct((2, 2 * bins, BAND), jnp.float32),
        in_specs=[pl.BlockSpec(memory_space=pltpu.SMEM)] + [whole(x.shape) for x in operands],
        out_specs=whole((2, 2 * bins, BAND)),
        scratch_shapes=[pltpu.VMEM((2, bins, TBLK), jnp.float32)],
        compiler_params=pltpu.CompilerParams(vmem_limit_bytes=62 * MIB),
        name="finish",
    )(meta, *operands)


def skew_rows(matrix, keep):
    height, width = matrix.shape
    flat = jnp.pad(matrix.reshape(height * width), (0, height))
    return flat.reshape(height, width + 1)[:, :keep]


def pair_count(quality_ext, reach_own, band):
    channel_count = reach_own.shape[0]
    ext_len = quality_ext.shape[0]
    partner = skew_rows(jnp.broadcast_to(quality_ext[None, :], (channel_count, ext_len)), band)
    offsets = jnp.arange(band, dtype=jnp.int32)[None, :]
    inside = (offsets < reach_own[:, None]).astype(jnp.int32)
    weight = quality_ext[:channel_count, None] * partner * inside
    return jnp.maximum(jnp.sum(weight.astype(jnp.float32), axis=0), 1.0)


def on_device(strain, quality, offset_reach):
    ch, length = strain.shape
    both = 2 * ch
    assert both == TBLK and BAND == 2 * both
    n_chan, n_freq = lax.axis_size("chan"), lax.axis_size("freq")
    count_a = length // TBLK
    rk = TBLK // 2 // n_freq
    me, band = lax.axis_index("chan"), lax.axis_index("freq")
    core, chip = me % 2, me // 2

    def moved(x, target):
        pairs = []
        for c in range(n_chan):
            for f in range(n_freq):
                to = target(c, f)
                if 0 <= to[0] < n_chan and 0 <= to[1] < n_freq:
                    pairs.append((c * n_freq + f, to[0] * n_freq + to[1]))
        return lax.ppermute(x, ("chan", "freq"), pairs)

    tail, head = strain[:, length - 2 * TBLK :], strain[:, : 2 * TBLK]
    other = moved(strain, lambda c, f: (c ^ 1, f))
    halos = [
        moved(tail, lambda c, f: (c, f + 1)),
        moved(tail, lambda c, f: (c ^ 1, f + 1)),
        moved(head, lambda c, f: (c, f - 1)),
        moved(head, lambda c, f: (c ^ 1, f - 1)),
    ]

    quality_pad = jnp.pad(quality, (0, BAND + both))
    reach_pad = jnp.pad(offset_reach, (both, 0))
    quality_both = lax.dynamic_slice_in_dim(quality_pad, chip * both, both, 0)
    reach_own = lax.dynamic_slice_in_dim(reach_pad, (chip + 1) * both, both, 0)[:, None]
    reach_prev = lax.dynamic_slice_in_dim(reach_pad, chip * both, both, 0)[:, None]
    quality_ext = lax.dynamic_slice_in_dim(quality_pad, me * ch, ch + BAND, 0)
    count = pair_count(quality_ext, lax.dynamic_slice_in_dim(offset_reach, me * ch, ch, 0), BAND)

    meta = jnp.stack([core, band]).astype(jnp.int32)
    parts = spectra(
        meta, strain, other, halos, quality_both.astype(jnp.float32)[None, :], n_freq
    )
    own = [parts[0]]
    for d in range(1, n_freq):
        own.append(moved(parts[d], lambda c, f, d=d: (c, f ^ d)))
    nxt = [moved(x, lambda c, f: (c - 2, f)) for x in own]
    prev = [moved(x, lambda c, f: (c + 2, f)) for x in own]
    near, far = cross(own, prev, nxt, reach_own, reach_prev, count_a, rk)
    nb = block_bins(n_freq)
    steps = far.shape[0] // (4 * nb)
    far = far.reshape(steps, 2, 2 * nb, both)
    pick = lambda x, axis, at: lax.dynamic_index_in_dim(x, at, axis, keepdims=False)
    theirs = moved(pick(near, 0, 1 - core), lambda c, f: (c ^ 1, f))
    far_a = moved(pick(far, 1, core).reshape(-1, both), lambda c, f: (c - 2, f))
    far_b = moved(pick(far, 1, 1 - core).reshape(-1, both), lambda c, f: ((c ^ 1) - 2, f))
    mine = pick(near, 0, core)
    out = finish(meta, mine, theirs, far_a, far_b, count[None, :], count_a, rk, nb)
    return out[None]


def solution(mesh):
    return jax.shard_map(
        on_device,
        mesh=mesh,
        in_specs=(P("chan", "freq"), P(), P()),
        out_specs=P("chan", None, "freq", None),
        check_vma=False,
    )
```

```python
import functools
import math

import jax
import jax.numpy as jnp
import ml_dtypes
import numpy as np
from jax import lax
from jax.experimental import pallas as pl
from jax.experimental.pallas import tpu as pltpu
from jax.sharding import PartitionSpec as P

BAND = 256
TBLK = 128

band_low = 0.004
band_high = 0.48
level_eps = 1e-05
MIB = 1 << 20


def tap_values(offset, half_span):
    window = 0.5 + 0.5 * np.cos(np.pi * offset / (half_span + 1))
    response = 2.0 * band_high * np.sinc(2.0 * band_high * offset) - 2.0 * band_low * np.sinc(
        2.0 * band_low * offset
    )
    return np.where(np.abs(offset) <= half_span, window * response, 0.0)


def stencil_table(boxed):
    offset = np.arange(2 * TBLK)[None, :] + TBLK - np.arange(4 * TBLK)[:, None]
    if boxed:
        values = np.where(np.abs(offset) <= TBLK, 1.0, 0.0)
    else:
        values = tap_values(offset.astype(np.float64), TBLK)
    return values.astype(ml_dtypes.bfloat16)


def dft_tables(count_a, n_freq):
    pad_a = -(-count_a // 16) * 16
    length = count_a * TBLK
    index = np.arange(count_a)
    angle = (index[:, None] * index[None, :] % count_a) * (2.0 * np.pi / count_a)
    first = np.zeros((2, pad_a, pad_a))
    first[0, :count_a, :count_a] = np.cos(angle)
    first[1, :count_a, :count_a] = -np.sin(angle)
    first = first.reshape(2 * pad_a, pad_a).astype(ml_dtypes.bfloat16)
    twist = np.zeros((2, pad_a, TBLK), np.float32)
    turn = (index[:, None] * np.arange(TBLK)[None, :] % length) * (2.0 * np.pi / length)
    twist[0, :count_a] = np.cos(turn)
    twist[1, :count_a] = np.sin(turn)
    k2_count = TBLK // 2
    turn = (np.arange(k2_count)[:, None] * np.arange(TBLK)[None, :] % TBLK) * (2.0 * np.pi / TBLK)
    real = np.concatenate([np.cos(turn), np.sin(turn)], axis=1)
    imag = np.concatenate([-np.sin(turn), np.cos(turn)], axis=1)
    half = k2_count // n_freq // 2
    second = np.stack([real, imag]).reshape(2, n_freq, 2, half, 2 * TBLK)
    second = second.transpose(1, 2, 0, 3, 4).reshape(n_freq, 2, 2 * half, 2 * TBLK)
    return first, twist, second.astype(ml_dtypes.bfloat16)


def block_bins(n_freq):
    return 16 if n_freq <= 4 else 8


def whole(shape):
    return pl.BlockSpec(shape, lambda t: (0,) * len(shape))


def spectra_kernel(
    count_a,
    n_freq,
    chunks,
    meta,
    own,
    other,
    lo_own,
    lo_other,
    hi_own,
    hi_other,
    taps,
    box,
    first,
    twist,
    second,
    quality,
    *rest,
):
    outs = rest[: n_freq * len(chunks)]
    padded, filtered, magnitude, whitened, tw_re, tw_im = rest[len(outs) :]
    core, band = meta[0], meta[1]
    ch = own.shape[0]
    both = 2 * ch
    pad_a = first.shape[1]
    dot = functools.partial(jnp.dot, preferred_element_type=jnp.float32)

    for which, (lo, mid, hi) in enumerate(((lo_own, own, hi_own), (lo_other, other, hi_other))):
        base = core if which == 0 else 1 - core
        rows = pl.ds(pl.multiple_of(base * ch, ch), ch)
        for j in range(2):
            padded[j, rows, :] = lo[:, j * TBLK : (j + 1) * TBLK]
            padded[count_a + 2 + j, rows, :] = hi[:, j * TBLK : (j + 1) * TBLK]
        for j in range(count_a):
            padded[2 + j, rows, :] = mid[:, j * TBLK : (j + 1) * TBLK]

    def fir(i, carry):
        j = 2 * i
        window = jnp.concatenate([padded[j + n] for n in range(4)], axis=1)
        result = dot(window, taps[...])
        for n in range(2):
            part = result[:, n * TBLK : (n + 1) * TBLK]
            filtered[j + n] = part
            magnitude[j + n] = jnp.abs(part).astype(jnp.bfloat16)
        return carry

    lax.fori_loop(0, count_a // 2 + 1, fir, 0, unroll=True)

    def whiten(i, carry):
        j = 2 * i
        window = jnp.concatenate([magnitude[j + n] for n in range(4)], axis=1)
        level = dot(window, box[...]) / (2 * TBLK + 1)
        for n in range(2):
            part = filtered[j + n + 1] / (level[:, n * TBLK : (n + 1) * TBLK] + level_eps)
            rows = pl.ds(pl.multiple_of((j + n) * both, both), both)
            whitened[rows, :] = part
        return carry

    lax.fori_loop(0, count_a // 2, whiten, 0, unroll=True)
    whitened[count_a * both : pad_a * both, :] = jnp.zeros(
        ((pad_a - count_a) * both, TBLK), jnp.float32
    )

    def sections(i, carry):
        c = 2 * i
        pair = [
            whitened[pl.ds(c + n, pad_a, stride=both), :].astype(jnp.bfloat16) for n in range(2)
        ]
        section = dot(first[...], jnp.concatenate(pair, axis=1))
        for n in range(2):
            re = section[:pad_a, n * TBLK : (n + 1) * TBLK]
            im = section[pad_a:, n * TBLK : (n + 1) * TBLK]
            rows = pl.ds(pl.multiple_of((c + n) * pad_a, pad_a), pad_a)
            tw_re[rows, :] = re * twist[0] + im * twist[1]
            tw_im[rows, :] = im * twist[0] - re * twist[1]
        return carry

    lax.fori_loop(0, both // 2, sections, 0, unroll=True)

    rk = second.shape[2]
    half = rk // 2
    group = block_bins(n_freq) // half
    scale = quality[...] * (1.0 / math.sqrt(count_a * TBLK))
    turn = jnp.concatenate([second[band ^ d, core] for d in range(n_freq)], axis=0)

    def bins(k, start, i):
        results = []
        for n in range(group):
            k1 = (start + i) * group + n
            re = tw_re[pl.ds(k1, both, stride=pad_a), :].astype(jnp.bfloat16)
            im = tw_im[pl.ds(k1, both, stride=pad_a), :].astype(jnp.bfloat16)
            result = lax.dot_general(
                turn,
                jnp.concatenate([re, im], axis=1),
                (((1,), (1,)), ((), ())),
                preferred_element_type=jnp.float32,
            )
            results.append(result * scale)
        rows = pl.ds(i * group * rk, group * rk)
        for d in range(n_freq):
            starts = [d * rk + p * half for p in range(2)]
            block = jnp.concatenate([r[s : s + half] for s in starts for r in results], axis=0)
            outs[k * n_freq + d][rows, :] = block.astype(jnp.bfloat16)

    start = 0
    for k, size in enumerate(chunks):
        for i in range(size):
            bins(k, start, i)
        start += size


def spectra(meta, own, other, halos, quality, n_freq, chunks):
    ch, length = own.shape
    count_a = length // TBLK
    first, twist, second = dft_tables(count_a, n_freq)
    rk = second.shape[2]
    pad_a = first.shape[1]
    both = 2 * ch
    rows = 2 * block_bins(n_freq)
    shapes = [(size * rows, both) for size in chunks for _ in range(n_freq)]
    tables = (stencil_table(False), stencil_table(True), first, twist, second)
    operands = (own, other, *halos, *(jnp.asarray(t) for t in tables), quality)
    return pl.pallas_call(
        functools.partial(spectra_kernel, count_a, n_freq, chunks),
        grid=(1,),
        out_shape=[jax.ShapeDtypeStruct(shape, jnp.bfloat16) for shape in shapes],
        in_specs=[pl.BlockSpec(memory_space=pltpu.SMEM)] + [whole(x.shape) for x in operands],
        out_specs=[whole(shape) for shape in shapes],
        scratch_shapes=[
            pltpu.VMEM((count_a + 4, both, TBLK), jnp.bfloat16),
            pltpu.VMEM((count_a + 2, both, TBLK), jnp.float32),
            pltpu.VMEM((count_a + 2, both, TBLK), jnp.bfloat16),
            pltpu.VMEM((pad_a * both, TBLK), jnp.float32),
            pltpu.VMEM((both * pad_a, TBLK), jnp.float32),
            pltpu.VMEM((both * pad_a, TBLK), jnp.float32),
        ],
        compiler_params=pltpu.CompilerParams(vmem_limit_bytes=62 * MIB),
        cost_estimate=pl.CostEstimate(
            flops=6 * 10**9, bytes_accessed=4 * 10**6, transcendentals=0
        ),
        name="spectra",
    )(meta, *operands)


def cross_kernel(
    meta,
    reach_own,
    reach_prev,
    turn_ref,
    pick_ref,
    cut_ref,
    own_ref,
    prev_ref,
    next_ref,
    mine_ref,
    theirs_ref,
    far_mine_ref,
    far_theirs_ref,
    w_near,
    w_far,
    edge,
    sum_one,
    sum_two,
    sum_far,
):
    step = pl.program_id(0)
    n_seg, rb, both = own_ref.shape
    depth = turn_ref.shape[0]
    nb = pick_ref.shape[0]
    slabs = both // 8
    first_core = meta[0] == 0

    @pl.when(step == 0)
    def _():
        row = lax.broadcasted_iota(jnp.int32, (16, both), 0) % 8
        col = lax.broadcasted_iota(jnp.int32, (16, both), 1)
        offset = (both + col - row).astype(jnp.float32)
        columns = [
            jnp.broadcast_to(r[...], (both, both)).T for r in (reach_own, reach_prev)
        ]
        wide = jnp.concatenate([columns[1], columns[1]], axis=1)
        for a in range(slabs):
            mine = columns[0][a * 8 : a * 8 + 8]
            lent = columns[1][a * 8 : a * 8 + 8]
            mine = jnp.concatenate([mine, mine], axis=0)
            lent = jnp.concatenate([lent, lent], axis=0)
            inner = col < both - 8 * a
            w_near[a] = jnp.where(inner & ((col < row) | (offset < mine)), 1.0, 0.0)
            w_far[a] = jnp.where(~inner & (offset < lent), 1.0, 0.0)
        row = lax.broadcasted_iota(jnp.int32, (both, 2 * both), 0)
        col = lax.broadcasted_iota(jnp.int32, (both, 2 * both), 1)
        same = (row // (both // 2)) == (col // both)
        for d in range(1, 8):
            hit = same & (col % both == both - d) & (row % 8 >= d)
            hit = hit & (2 * both - d < wide)
            edge[(d - 1) * both : d * both, :] = jnp.where(hit, 1.0, 0.0).astype(jnp.bfloat16)

    def left_rows(block):
        re = block.astype(jnp.float32).T.astype(jnp.bfloat16)
        im = jnp.dot(re, turn_ref[...], preferred_element_type=jnp.float32)
        re = re.astype(jnp.float32).reshape(slabs, 8, depth)
        im = im.reshape(slabs, 8, depth)
        return jnp.stack([re, im], axis=1).reshape(slabs, 16, depth).astype(jnp.bfloat16)

    own, nxt, prev = (r[...].reshape(depth, both) for r in (own_ref, next_ref, prev_ref))
    left = jnp.concatenate([left_rows(own), left_rows(prev)], axis=2)
    pick = pick_ref[...]

    zero = jnp.zeros_like(own)
    for a in range(slabs):
        g, first = divmod(a, slabs // 2)
        if a == 0:
            right = jnp.concatenate(
                [jnp.concatenate([own, nxt], axis=1), jnp.concatenate([zero, zero], axis=1)],
                axis=0,
            )
        else:
            moved_own = pltpu.roll(own, both - 8 * a, 1).reshape(depth // 16, 16, both)
            moved_next = pltpu.roll(nxt, both - 8 * a, 1).reshape(depth // 16, 16, both)
            cut = cut_ref[a][None]
            inner = moved_next * cut
            outer = moved_next - inner
            local = (moved_own * cut + outer).reshape(depth, both)
            inner = inner.reshape(depth, both)
            outer = outer.reshape(depth, both)
            right = jnp.concatenate(
                [
                    jnp.concatenate([local, inner], axis=1),
                    jnp.concatenate([zero, outer], axis=1),
                ],
                axis=0,
            )
        rows = (left[a][None] * pick).reshape(nb * 16, 2 * depth)
        result = jnp.dot(rows, right, preferred_element_type=jnp.float32)
        one = result[:, :both]
        two = result[:, both:].reshape(nb, 16, both)
        near = (two * w_near[a][None]).reshape(nb * 16, both)
        far = (two * w_far[a][None]).reshape(nb * 16, both)
        if first == 0:
            sum_one[g], sum_two[g], sum_far[g] = one, near, far
        else:
            sum_one[g] += one
            sum_two[g] += near
            sum_far[g] += far

    def split(x):
        return x[:nb], x[nb:]

    lefts = [split(prev_ref[s].astype(jnp.float32)) for s in range(n_seg)]
    rights = [split(next_ref[s].astype(jnp.float32)) for s in range(n_seg)]
    pieces = []
    for d in range(1, 8):
        re = im = None
        for (xr, xi), (yr, yi) in zip(lefts, rights):
            yr, yi = pltpu.roll(yr, d, 1), pltpu.roll(yi, d, 1)
            r, i = xr * yr + xi * yi, xi * yr - xr * yi
            re, im = (r, i) if re is None else (re + r, im + i)
        pieces.append(jnp.concatenate([re, im], axis=0).astype(jnp.bfloat16))
    margin = jnp.dot(
        jnp.concatenate(pieces, axis=1), edge[...], preferred_element_type=jnp.float32
    )

    lane = lax.broadcasted_iota(jnp.int32, (nb, both), 1)
    for p in range(2):
        values = []
        for g in range(2):
            low = high = far = None
            for b in range(8):
                rows = pl.ds(p * 8 + b, nb, stride=16)
                one, two, three = sum_one[g, rows, :], sum_two[g, rows, :], sum_far[g, rows, :]
                if b == 0:
                    low, high, far = one, two, three
                    continue
                low += pltpu.roll(jnp.where(lane >= b, one, two), both - b, 1)
                high += pltpu.roll(jnp.where(lane >= b, two, 0.0), both - b, 1)
                far += pltpu.roll(three, both - b, 1)
            far += margin[p * nb : (p + 1) * nb, g * both : (g + 1) * both]
            values.append((low, high, far))
        mine = [jnp.where(first_core, x, y) for x, y in zip(*values)]
        theirs = [jnp.where(first_core, y, x) for x, y in zip(*values)]
        for near_ref, far_ref, value in (
            (mine_ref, far_mine_ref, mine),
            (theirs_ref, far_theirs_ref, theirs),
        ):
            near_ref[p, 0, :nb] = value[0]
            near_ref[p, 0, nb:] = value[1]
            far_ref[p, 0] = value[2].astype(jnp.bfloat16)


def cross(meta, own, prev, nxt, reach_own, reach_prev):
    n_seg, rows, both = own.shape
    nb = block_bins(n_seg)
    rb = 2 * nb
    depth = n_seg * rb
    steps = rows // rb
    slabs = both // 8
    lane = np.arange(depth)
    part = lane % rb // nb
    turn = np.zeros((depth, depth))
    turn[lane + np.where(part == 0, nb, -nb), lane] = np.where(part == 0, 1.0, -1.0)
    lane = np.arange(2 * depth)
    pick = (lane % nb == np.arange(nb)[:, None, None]).astype(np.float32)
    pick = np.broadcast_to(pick, (nb, 16, 2 * depth))
    cut = np.arange(both) < both - 8 * np.arange(slabs)[:, None, None]
    cut = np.broadcast_to(cut, (slabs, 16, both))
    tables = [jnp.asarray(x.astype(ml_dtypes.bfloat16)) for x in (turn, pick, cut)]
    fixed = (reach_own, reach_prev, *tables)
    near = jax.ShapeDtypeStruct((2, steps, 2 * nb, both), jnp.float32)
    far = jax.ShapeDtypeStruct((2, steps, nb, both), jnp.bfloat16)
    near_spec = pl.BlockSpec((2, 1, 2 * nb, both), lambda t: (0, t, 0, 0))
    far_spec = pl.BlockSpec((2, 1, nb, both), lambda t: (0, t, 0, 0))
    block = pl.BlockSpec((n_seg, rb, both), lambda t: (0, t, 0))
    return pl.pallas_call(
        cross_kernel,
        grid=(steps,),
        out_shape=[near, near, far, far],
        in_specs=[pl.BlockSpec(memory_space=pltpu.SMEM)]
        + [whole(x.shape) for x in fixed]
        + [block] * 3,
        out_specs=[near_spec, near_spec, far_spec, far_spec],
        scratch_shapes=[
            pltpu.VMEM((slabs, 16, both), jnp.float32),
            pltpu.VMEM((slabs, 16, both), jnp.float32),
            pltpu.VMEM((7 * both, 2 * both), jnp.bfloat16),
            pltpu.VMEM((2, nb * 16, both), jnp.float32),
            pltpu.VMEM((2, nb * 16, both), jnp.float32),
            pltpu.VMEM((2, nb * 16, both), jnp.float32),
        ],
        compiler_params=pltpu.CompilerParams(
            dimension_semantics=("arbitrary",), vmem_limit_bytes=62 * MIB
        ),
        cost_estimate=pl.CostEstimate(
            flops=10**9 * steps, bytes_accessed=2 * 10**5 * steps, transcendentals=0
        ),
        name="cross",
    )(meta, *fixed, own, prev, nxt)


def finish_kernel(count_a, half, chunks, meta, count, *rest):
    parts, out_ref, stage = rest[: 4 * chunks], rest[4 * chunks], rest[4 * chunks + 1]
    core = meta[0]
    bins = out_ref.shape[1] // 2
    inverse = 1.0 / count[...]
    k1 = 0
    for chunk in range(chunks):
        mine, theirs, far_mine, far_theirs = parts[4 * chunk : 4 * chunk + 4]
        steps, nb, both = far_mine.shape[1:]
        for t in range(steps):
            for which, (near, far) in enumerate(((mine, far_mine), (theirs, far_theirs))):
                base = (core if which == 0 else 1 - core) * bins
                value = near[0, t]
                low = value[:nb] * inverse[:, :both]
                high = (value[nb:] + far[0, t].astype(jnp.float32)) * inverse[:, both:]
                for r, x in enumerate((low, high)):
                    for n in range(nb // half):
                        place = pl.ds(base + k1 + n, half, stride=count_a)
                        stage[r, place, :] = x[n * half : (n + 1) * half]
            k1 += nb // half
    for r in range(2):
        both = stage.shape[2]
        out_ref[0, :, r * both : (r + 1) * both] = stage[r]


def finish(meta, count, parts, count_a, half):
    bins = count_a * half

    def half_of(shape):
        return pl.BlockSpec((1,) + shape[1:], lambda p: (p,) + (0,) * (len(shape) - 1))

    return pl.pallas_call(
        functools.partial(finish_kernel, count_a, half, len(parts) // 4),
        grid=(2,),
        out_shape=jax.ShapeDtypeStruct((2, 2 * bins, BAND), jnp.float32),
        in_specs=[pl.BlockSpec(memory_space=pltpu.SMEM), whole(count.shape)]
        + [half_of(x.shape) for x in parts],
        out_specs=half_of((2, 2 * bins, BAND)),
        scratch_shapes=[pltpu.VMEM((2, 2 * bins, TBLK), jnp.float32)],
        compiler_params=pltpu.CompilerParams(vmem_limit_bytes=62 * MIB),
        name="finish",
    )(meta, count, *parts)


def skew_rows(matrix, keep):
    height, width = matrix.shape
    flat = jnp.pad(matrix.reshape(height * width), (0, height))
    return flat.reshape(height, width + 1)[:, :keep]


def pair_count(quality_ext, reach_own, band):
    channel_count = reach_own.shape[0]
    ext_len = quality_ext.shape[0]
    partner = skew_rows(jnp.broadcast_to(quality_ext[None, :], (channel_count, ext_len)), band)
    offsets = jnp.arange(band, dtype=jnp.int32)[None, :]
    inside = (offsets < reach_own[:, None]).astype(jnp.int32)
    weight = quality_ext[:channel_count, None] * partner * inside
    return jnp.maximum(jnp.sum(weight.astype(jnp.float32), axis=0), 1.0)


def on_device(strain, quality, offset_reach):
    ch, length = strain.shape
    both = 2 * ch
    assert both == TBLK and BAND == 2 * both
    n_chan, n_freq = lax.axis_size("chan"), lax.axis_size("freq")
    count_a = length // TBLK
    rk = TBLK // 2 // n_freq
    me, band = lax.axis_index("chan"), lax.axis_index("freq")
    core, chip = me % 2, me // 2

    def moved(x, target):
        pairs = []
        for c in range(n_chan):
            for f in range(n_freq):
                to = target(c, f)
                if 0 <= to[0] < n_chan and 0 <= to[1] < n_freq:
                    pairs.append((c * n_freq + f, to[0] * n_freq + to[1]))
        return lax.ppermute(x, ("chan", "freq"), pairs)

    tail, head = strain[:, length - 2 * TBLK :], strain[:, : 2 * TBLK]
    other = moved(strain, lambda c, f: (c ^ 1, f))
    halos = [
        moved(tail, lambda c, f: (c, f + 1)),
        moved(tail, lambda c, f: (c ^ 1, f + 1)),
        moved(head, lambda c, f: (c, f - 1)),
        moved(head, lambda c, f: (c ^ 1, f - 1)),
    ]

    quality_pad = jnp.pad(quality, (0, BAND + both))
    reach_pad = jnp.pad(offset_reach, (both, 0))
    quality_both = lax.dynamic_slice_in_dim(quality_pad, chip * both, both, 0)
    reach_pad = reach_pad.astype(jnp.float32)
    reach_own = lax.dynamic_slice_in_dim(reach_pad, (chip + 1) * both, both, 0)[None, :]
    reach_prev = lax.dynamic_slice_in_dim(reach_pad, chip * both, both, 0)[None, :]
    quality_ext = lax.dynamic_slice_in_dim(quality_pad, me * ch, ch + BAND, 0)
    count = pair_count(quality_ext, lax.dynamic_slice_in_dim(offset_reach, me * ch, ch, 0), BAND)

    meta = jnp.stack([core, band]).astype(jnp.int32)
    half = rk // 2
    steps = count_a * half // block_bins(n_freq)
    chunks = (steps // 2, steps - steps // 2)
    pieces = spectra(
        meta, strain, other, halos, quality_both.astype(jnp.float32)[None, :], n_freq, chunks
    )
    blocks = []
    for k in range(len(chunks)):
        mine = pieces[k * n_freq : (k + 1) * n_freq]
        own = [mine[0]]
        for d in range(1, n_freq):
            own.append(moved(mine[d], lambda c, f, d=d: (c, f ^ d)))
        blocks.append(jnp.stack(own))
    results = []
    for own in blocks:
        nxt = moved(own, lambda c, f: (c - 2, f))
        prev = moved(own, lambda c, f: (c + 2, f))
        mine, theirs, far_mine, far_theirs = cross(meta, own, prev, nxt, reach_own, reach_prev)
        results += [
            mine,
            moved(theirs, lambda c, f: (c ^ 1, f)),
            moved(far_mine, lambda c, f: (c - 2, f)),
            moved(far_theirs, lambda c, f: ((c ^ 1) - 2, f)),
        ]
    return finish(meta, count[None, :], results, count_a, half)[None]


def solution(mesh):
    return jax.shard_map(
        on_device,
        mesh=mesh,
        in_specs=(P("chan", "freq"), P(), P()),
        out_specs=P("chan", None, "freq", None),
        check_vma=False,
    )
```

```python
import functools
import math

import jax
import jax.numpy as jnp
import ml_dtypes
import numpy as np
from jax import lax
from jax.experimental import pallas as pl
from jax.experimental.pallas import tpu as pltpu
from jax.sharding import PartitionSpec as P

BAND = 256
TBLK = 128

band_low = 0.004
band_high = 0.48
level_eps = 1e-05
MIB = 1 << 20


def tap_values(offset, half_span):
    window = 0.5 + 0.5 * np.cos(np.pi * offset / (half_span + 1))
    response = 2.0 * band_high * np.sinc(2.0 * band_high * offset) - 2.0 * band_low * np.sinc(
        2.0 * band_low * offset
    )
    return np.where(np.abs(offset) <= half_span, window * response, 0.0)


def stencil_table(boxed):
    offset = np.arange(2 * TBLK)[None, :] + TBLK - np.arange(4 * TBLK)[:, None]
    if boxed:
        values = np.where(np.abs(offset) <= TBLK, 1.0, 0.0)
    else:
        values = tap_values(offset.astype(np.float64), TBLK)
    return values.astype(ml_dtypes.bfloat16)


def dft_tables(count_a, n_freq):
    pad_a = -(-count_a // 16) * 16
    length = count_a * TBLK
    index = np.arange(count_a)
    angle = (index[:, None] * index[None, :] % count_a) * (2.0 * np.pi / count_a)
    first = np.zeros((2, pad_a, pad_a))
    first[0, :count_a, :count_a] = np.cos(angle)
    first[1, :count_a, :count_a] = -np.sin(angle)
    first = first.reshape(2 * pad_a, pad_a).astype(ml_dtypes.bfloat16)
    twist = np.zeros((2, pad_a, TBLK), np.float32)
    turn = (index[:, None] * np.arange(TBLK)[None, :] % length) * (2.0 * np.pi / length)
    twist[0, :count_a] = np.cos(turn)
    twist[1, :count_a] = np.sin(turn)
    k2_count = TBLK // 2
    turn = (np.arange(k2_count)[:, None] * np.arange(TBLK)[None, :] % TBLK) * (2.0 * np.pi / TBLK)
    real = np.concatenate([np.cos(turn), np.sin(turn)], axis=1)
    imag = np.concatenate([-np.sin(turn), np.cos(turn)], axis=1)
    half = k2_count // n_freq // 2
    second = np.stack([real, imag]).reshape(2, n_freq, 2, half, 2 * TBLK)
    second = second.transpose(1, 2, 0, 3, 4).reshape(n_freq, 2, 2 * half, 2 * TBLK)
    return first, twist, second.astype(ml_dtypes.bfloat16)


def block_bins(n_freq):
    return 16 if n_freq <= 4 else 8


def whole(shape):
    return pl.BlockSpec(shape, lambda t: (0,) * len(shape))


def spectra_kernel(
    count_a,
    n_freq,
    own,
    other,
    lo_own,
    lo_other,
    hi_own,
    hi_other,
    taps,
    box,
    first,
    twist,
    second,
    *rest,
):
    outs = rest[:n_freq]
    padded, filtered, magnitude, whitened, tw_re, tw_im = rest[len(outs) :]
    core, band = lax.axis_index("chan") % 2, lax.axis_index("freq")
    ch = own.shape[0]
    both = 2 * ch
    pad_a = first.shape[1]
    dot = functools.partial(jnp.dot, preferred_element_type=jnp.float32)

    for which, (lo, mid, hi) in enumerate(((lo_own, own, hi_own), (lo_other, other, hi_other))):
        base = core if which == 0 else 1 - core
        rows = pl.ds(pl.multiple_of(base * ch, ch), ch)
        for j in range(2):
            padded[j, rows, :] = lo[:, j * TBLK : (j + 1) * TBLK]
            padded[count_a + 2 + j, rows, :] = hi[:, j * TBLK : (j + 1) * TBLK]
        for j in range(count_a):
            padded[2 + j, rows, :] = mid[:, j * TBLK : (j + 1) * TBLK]

    def fir(i, carry):
        j = 2 * i
        window = jnp.concatenate([padded[j + n] for n in range(4)], axis=1)
        result = dot(window, taps[...])
        for n in range(2):
            part = result[:, n * TBLK : (n + 1) * TBLK]
            filtered[j + n] = part
            magnitude[j + n] = jnp.abs(part).astype(jnp.bfloat16)
        return carry

    lax.fori_loop(0, count_a // 2 + 1, fir, 0, unroll=True)

    def whiten(i, carry):
        j = 2 * i
        window = jnp.concatenate([magnitude[j + n] for n in range(4)], axis=1)
        level = dot(window, box[...]) / (2 * TBLK + 1)
        for n in range(2):
            part = filtered[j + n + 1] / (level[:, n * TBLK : (n + 1) * TBLK] + level_eps)
            rows = pl.ds(pl.multiple_of((j + n) * both, both), both)
            whitened[rows, :] = part
        return carry

    lax.fori_loop(0, count_a // 2, whiten, 0, unroll=True)
    whitened[count_a * both : pad_a * both, :] = jnp.zeros(
        ((pad_a - count_a) * both, TBLK), jnp.float32
    )

    def sections(i, carry):
        c = 2 * i
        pair = [
            whitened[pl.ds(c + n, pad_a, stride=both), :].astype(jnp.bfloat16) for n in range(2)
        ]
        section = dot(first[...], jnp.concatenate(pair, axis=1))
        for n in range(2):
            re = section[:pad_a, n * TBLK : (n + 1) * TBLK]
            im = section[pad_a:, n * TBLK : (n + 1) * TBLK]
            rows = pl.ds(pl.multiple_of((c + n) * pad_a, pad_a), pad_a)
            tw_re[rows, :] = re * twist[0] + im * twist[1]
            tw_im[rows, :] = im * twist[0] - re * twist[1]
        return carry

    lax.fori_loop(0, both // 2, sections, 0, unroll=True)

    rk = second.shape[2]
    half = rk // 2
    group = block_bins(n_freq) // half
    scale = 1.0 / math.sqrt(count_a * TBLK)
    turn = jnp.concatenate([second[band ^ d, core] for d in range(n_freq)], axis=0)

    def bins(i):
        results = []
        for n in range(group):
            k1 = i * group + n
            re = tw_re[pl.ds(k1, both, stride=pad_a), :].astype(jnp.bfloat16)
            im = tw_im[pl.ds(k1, both, stride=pad_a), :].astype(jnp.bfloat16)
            result = lax.dot_general(
                turn,
                jnp.concatenate([re, im], axis=1),
                (((1,), (1,)), ((), ())),
                preferred_element_type=jnp.float32,
            )
            results.append(result * scale)
        rows = pl.ds(i * group * rk, group * rk)
        for d in range(n_freq):
            starts = [d * rk + p * half for p in range(2)]
            block = jnp.concatenate([r[s : s + half] for s in starts for r in results], axis=0)
            outs[d][rows, :] = block.astype(jnp.bfloat16)

    for i in range(count_a // group):
        bins(i)


def spectra(own, other, halos, n_freq):
    ch, length = own.shape
    count_a = length // TBLK
    first, twist, second = dft_tables(count_a, n_freq)
    rk = second.shape[2]
    pad_a = first.shape[1]
    both = 2 * ch
    shapes = [(count_a * rk, both)] * n_freq
    tables = (stencil_table(False), stencil_table(True), first, twist, second)
    operands = (own, other, *halos, *(jnp.asarray(t) for t in tables))
    return pl.pallas_call(
        functools.partial(spectra_kernel, count_a, n_freq),
        grid=(1,),
        out_shape=[jax.ShapeDtypeStruct(shape, jnp.bfloat16) for shape in shapes],
        in_specs=[whole(x.shape) for x in operands],
        out_specs=[whole(shape) for shape in shapes],
        scratch_shapes=[
            pltpu.VMEM((count_a + 4, both, TBLK), jnp.bfloat16),
            pltpu.VMEM((count_a + 2, both, TBLK), jnp.float32),
            pltpu.VMEM((count_a + 2, both, TBLK), jnp.bfloat16),
            pltpu.VMEM((pad_a * both, TBLK), jnp.float32),
            pltpu.VMEM((both * pad_a, TBLK), jnp.float32),
            pltpu.VMEM((both * pad_a, TBLK), jnp.float32),
        ],
        compiler_params=pltpu.CompilerParams(vmem_limit_bytes=62 * MIB),
        cost_estimate=pl.CostEstimate(
            flops=6 * 10**9, bytes_accessed=4 * 10**6, transcendentals=0
        ),
        name="spectra",
    )(*operands)


def cross_kernel(
    per,
    reach_own,
    reach_prev,
    turn_ref,
    pick_ref,
    cut_ref,
    own_ref,
    prev_ref,
    next_ref,
    mine_ref,
    theirs_ref,
    far_mine_ref,
    far_theirs_ref,
    w_near,
    w_far,
    edge,
    sum_one,
    sum_two,
    sum_far,
):
    step = pl.program_id(0)
    n_seg, rb, both = own_ref.shape
    rb //= per
    depth = turn_ref.shape[0]
    nb = pick_ref.shape[0]
    slabs = both // 8
    first_core = lax.axis_index("chan") % 2 == 0

    @pl.when(step == 0)
    def _():
        row = lax.broadcasted_iota(jnp.int32, (16, both), 0) % 8
        col = lax.broadcasted_iota(jnp.int32, (16, both), 1)
        offset = (both + col - row).astype(jnp.float32)
        columns = [
            jnp.broadcast_to(r[...], (both, both)).T for r in (reach_own, reach_prev)
        ]
        wide = jnp.concatenate([columns[1], columns[1]], axis=1)
        for a in range(slabs):
            mine = columns[0][a * 8 : a * 8 + 8]
            lent = columns[1][a * 8 : a * 8 + 8]
            mine = jnp.concatenate([mine, mine], axis=0)
            lent = jnp.concatenate([lent, lent], axis=0)
            inner = col < both - 8 * a
            w_near[a] = jnp.where(inner & ((col < row) | (offset < mine)), 1.0, 0.0)
            w_far[a] = jnp.where(~inner & (offset < lent), 1.0, 0.0)
        row = lax.broadcasted_iota(jnp.int32, (both, 2 * both), 0)
        col = lax.broadcasted_iota(jnp.int32, (both, 2 * both), 1)
        same = (row // (both // 2)) == (col // both)
        for d in range(1, 8):
            hit = same & (col % both == both - d) & (row % 8 >= d)
            hit = hit & (2 * both - d < wide)
            edge[(d - 1) * both : d * both, :] = jnp.where(hit, 1.0, 0.0).astype(jnp.bfloat16)

    def left_rows(block):
        re = block.astype(jnp.float32).T.astype(jnp.bfloat16)
        im = jnp.dot(re, turn_ref[...], preferred_element_type=jnp.float32)
        re = re.astype(jnp.float32).reshape(slabs, 8, depth)
        im = im.reshape(slabs, 8, depth)
        return jnp.stack([re, im], axis=1).reshape(slabs, 16, depth).astype(jnp.bfloat16)

    def dots(j):
        own, nxt, prev = (r[:, j * rb : (j + 1) * rb, :].reshape(depth, both) for r in (own_ref, next_ref, prev_ref))
        left = jnp.concatenate([left_rows(own), left_rows(prev)], axis=2)
        pick = pick_ref[...]

        zero = jnp.zeros_like(own)
        for a in range(slabs):
            g, first = divmod(a, slabs // 2)
            if a == 0:
                right = jnp.concatenate(
                    [jnp.concatenate([own, nxt], axis=1), jnp.concatenate([zero, zero], axis=1)],
                    axis=0,
                )
            else:
                moved_own = pltpu.roll(own, both - 8 * a, 1).reshape(depth // 16, 16, both)
                moved_next = pltpu.roll(nxt, both - 8 * a, 1).reshape(depth // 16, 16, both)
                cut = cut_ref[a][None]
                inner = moved_next * cut
                outer = moved_next - inner
                local = (moved_own * cut + outer).reshape(depth, both)
                inner = inner.reshape(depth, both)
                outer = outer.reshape(depth, both)
                right = jnp.concatenate(
                    [
                        jnp.concatenate([local, inner], axis=1),
                        jnp.concatenate([zero, outer], axis=1),
                    ],
                    axis=0,
                )
            rows = (left[a][None] * pick).reshape(nb * 16, 2 * depth)
            result = jnp.dot(rows, right, preferred_element_type=jnp.float32)
            one = result[:, :both]
            two = result[:, both:].reshape(nb, 16, both)
            near = (two * w_near[a][None]).reshape(nb * 16, both)
            far = (two * w_far[a][None]).reshape(nb * 16, both)
            if first == 0:
                sum_one[2 * j + g], sum_two[2 * j + g], sum_far[2 * j + g] = one, near, far
            else:
                sum_one[2 * j + g] += one
                sum_two[2 * j + g] += near
                sum_far[2 * j + g] += far


    def margins(j):
        def split(x):
            return x[:nb], x[nb:]

        lefts = [split(prev_ref[s, j * rb : (j + 1) * rb].astype(jnp.float32)) for s in range(n_seg)]
        rights = [split(next_ref[s, j * rb : (j + 1) * rb].astype(jnp.float32)) for s in range(n_seg)]
        pieces = []
        for d in range(1, 8):
            re = im = None
            for (xr, xi), (yr, yi) in zip(lefts, rights):
                yr, yi = pltpu.roll(yr, d, 1), pltpu.roll(yi, d, 1)
                r, i = xr * yr + xi * yi, xi * yr - xr * yi
                re, im = (r, i) if re is None else (re + r, im + i)
            pieces.append(jnp.concatenate([re, im], axis=0).astype(jnp.bfloat16))
        margin = jnp.dot(
            jnp.concatenate(pieces, axis=1), edge[...], preferred_element_type=jnp.float32
        )


        return margin

    def diag(j, margin):
        lane = lax.broadcasted_iota(jnp.int32, (nb, both), 1)
        for p in range(2):
            values = []
            for g in range(2):
                low = high = far = None
                for b in range(8):
                    rows = pl.ds(p * 8 + b, nb, stride=16)
                    one, two, three = sum_one[2 * j + g, rows, :], sum_two[2 * j + g, rows, :], sum_far[2 * j + g, rows, :]
                    if b == 0:
                        low, high, far = one, two, three
                        continue
                    low += pltpu.roll(jnp.where(lane >= b, one, two), both - b, 1)
                    high += pltpu.roll(jnp.where(lane >= b, two, 0.0), both - b, 1)
                    far += pltpu.roll(three, both - b, 1)
                far += margin[p * nb : (p + 1) * nb, g * both : (g + 1) * both]
                values.append((low, high, far))
            mine = [jnp.where(first_core, x, y) for x, y in zip(*values)]
            theirs = [jnp.where(first_core, y, x) for x, y in zip(*values)]
            for near_ref, far_ref, value in (
                (mine_ref, far_mine_ref, mine),
                (theirs_ref, far_theirs_ref, theirs),
            ):
                near_ref[p, j, :nb] = value[0]
                near_ref[p, j, nb:] = value[1]
                far_ref[p, j] = value[2].astype(far_ref.dtype)

    for j in range(per):
        dots(j)
    margin = [margins(j) for j in range(per)]
    for j in range(per):
        diag(j, margin[j])


def cross(own, prev, nxt, reach_own, reach_prev, far_type):
    n_seg, rows, both = own.shape
    nb = block_bins(n_seg)
    rb = 2 * nb
    depth = n_seg * rb
    steps = rows // rb
    slabs = both // 8
    per = 2 if steps % 2 == 0 else 1
    lane = np.arange(depth)
    part = lane % rb // nb
    turn = np.zeros((depth, depth))
    turn[lane + np.where(part == 0, nb, -nb), lane] = np.where(part == 0, 1.0, -1.0)
    lane = np.arange(2 * depth)
    pick = (lane % nb == np.arange(nb)[:, None, None]).astype(np.float32)
    pick = np.broadcast_to(pick, (nb, 16, 2 * depth))
    cut = np.arange(both) < both - 8 * np.arange(slabs)[:, None, None]
    cut = np.broadcast_to(cut, (slabs, 16, both))
    tables = [jnp.asarray(x.astype(ml_dtypes.bfloat16)) for x in (turn, pick, cut)]
    fixed = (reach_own, reach_prev, *tables)
    near = jax.ShapeDtypeStruct((2, steps, 2 * nb, both), jnp.float32)
    far = jax.ShapeDtypeStruct((2, steps, nb, both), far_type)
    near_spec = pl.BlockSpec((2, per, 2 * nb, both), lambda t: (0, t, 0, 0))
    far_spec = pl.BlockSpec((2, per, nb, both), lambda t: (0, t, 0, 0))
    block = pl.BlockSpec((n_seg, per * rb, both), lambda t: (0, t, 0))
    return pl.pallas_call(
        functools.partial(cross_kernel, per),
        grid=(steps // per,),
        out_shape=[near, near, far, far],
        in_specs=[whole(x.shape) for x in fixed] + [block] * 3,
        out_specs=[near_spec, near_spec, far_spec, far_spec],
        scratch_shapes=[
            pltpu.VMEM((slabs, 16, both), jnp.float32),
            pltpu.VMEM((slabs, 16, both), jnp.float32),
            pltpu.VMEM((7 * both, 2 * both), jnp.bfloat16),
            pltpu.VMEM((2 * per, nb * 16, both), jnp.float32),
            pltpu.VMEM((2 * per, nb * 16, both), jnp.float32),
            pltpu.VMEM((2 * per, nb * 16, both), jnp.float32),
        ],
        compiler_params=pltpu.CompilerParams(
            dimension_semantics=("arbitrary",), vmem_limit_bytes=24 * MIB
        ),
        cost_estimate=pl.CostEstimate(
            flops=10**9 * steps, bytes_accessed=2 * 10**5 * steps, transcendentals=0
        ),
        name="cross",
    )(*fixed, own, prev, nxt)


def finish_kernel(count_a, half, chunks, count, *rest):
    parts, out_ref, stage = rest[: 4 * chunks], rest[4 * chunks], rest[4 * chunks + 1]
    core = lax.axis_index("chan") % 2
    bins = out_ref.shape[1] // 2
    inverse = 1.0 / count[...]
    k1 = 0
    for chunk in range(chunks):
        mine, theirs, far_mine, far_theirs = parts[4 * chunk : 4 * chunk + 4]
        steps, nb, both = far_mine.shape[1:]
        for t in range(steps):
            for which, (near, far) in enumerate(((mine, far_mine), (theirs, far_theirs))):
                base = (core if which == 0 else 1 - core) * bins
                value = near[0, t]
                low = value[:nb] * inverse[:, :both]
                high = (value[nb:] + far[0, t].astype(jnp.float32)) * inverse[:, both:]
                for r, x in enumerate((low, high)):
                    for n in range(nb // half):
                        place = pl.ds(base + k1 + n, half, stride=count_a)
                        stage[r, place, :] = x[n * half : (n + 1) * half]
            k1 += nb // half
    for r in range(2):
        both = stage.shape[2]
        out_ref[0, :, r * both : (r + 1) * both] = stage[r]


def finish(count, parts, count_a, half):
    bins = count_a * half

    def half_of(shape):
        return pl.BlockSpec((1,) + shape[1:], lambda p: (p,) + (0,) * (len(shape) - 1))

    return pl.pallas_call(
        functools.partial(finish_kernel, count_a, half, len(parts) // 4),
        grid=(2,),
        out_shape=jax.ShapeDtypeStruct((2, 2 * bins, BAND), jnp.float32),
        in_specs=[whole(count.shape)] + [half_of(x.shape) for x in parts],
        out_specs=half_of((2, 2 * bins, BAND)),
        scratch_shapes=[pltpu.VMEM((2, 2 * bins, TBLK), jnp.float32)],
        compiler_params=pltpu.CompilerParams(vmem_limit_bytes=24 * MIB),
        name="finish",
    )(count, *parts)


def skew_rows(matrix, keep):
    height, width = matrix.shape
    flat = jnp.pad(matrix.reshape(height * width), (0, height))
    return flat.reshape(height, width + 1)[:, :keep]


def pair_count(quality_ext, reach_own, band):
    channel_count = reach_own.shape[0]
    ext_len = quality_ext.shape[0]
    partner = skew_rows(jnp.broadcast_to(quality_ext[None, :], (channel_count, ext_len)), band)
    offsets = jnp.arange(band, dtype=jnp.int32)[None, :]
    inside = (offsets < reach_own[:, None]).astype(jnp.int32)
    weight = quality_ext[:channel_count, None] * partner * inside
    return jnp.maximum(jnp.sum(weight.astype(jnp.float32), axis=0), 1.0)


def on_device(strain, quality, offset_reach):
    ch, length = strain.shape
    both = 2 * ch
    assert both == TBLK and BAND == 2 * both
    n_chan, n_freq = lax.axis_size("chan"), lax.axis_size("freq")
    count_a = length // TBLK
    rk = TBLK // 2 // n_freq
    me = lax.axis_index("chan")
    chip = me // 2

    def moved(x, target):
        pairs = []
        for c in range(n_chan):
            for f in range(n_freq):
                to = target(c, f)
                if 0 <= to[0] < n_chan and 0 <= to[1] < n_freq:
                    pairs.append((c * n_freq + f, to[0] * n_freq + to[1]))
        return lax.ppermute(x, ("chan", "freq"), pairs)

    tail, head = strain[:, length - 2 * TBLK :], strain[:, : 2 * TBLK]
    other = moved(strain, lambda c, f: (c ^ 1, f))
    halos = [
        moved(tail, lambda c, f: (c, f + 1)),
        moved(tail, lambda c, f: (c ^ 1, f + 1)),
        moved(head, lambda c, f: (c, f - 1)),
        moved(head, lambda c, f: (c ^ 1, f - 1)),
    ]

    quality_pad = jnp.pad(quality, (0, BAND + both))
    reach_pad = jnp.pad(offset_reach, (both, 0))
    quality_both = lax.dynamic_slice_in_dim(quality_pad, chip * both, both, 0)
    reach_pad = reach_pad.astype(jnp.float32)
    reach_own = lax.dynamic_slice_in_dim(reach_pad, (chip + 1) * both, both, 0)[None, :]
    reach_prev = lax.dynamic_slice_in_dim(reach_pad, chip * both, both, 0)[None, :]
    quality_ext = lax.dynamic_slice_in_dim(quality_pad, me * ch, ch + BAND, 0)
    count = pair_count(quality_ext, lax.dynamic_slice_in_dim(offset_reach, me * ch, ch, 0), BAND)

    half = rk // 2
    nb = block_bins(n_freq)
    steps = count_a * half // nb
    first = steps * 7 // 15
    chunks = (first, steps - first)
    parts = spectra(strain, other, halos, n_freq)
    pieces = [parts[0]]
    for d in range(1, n_freq):
        pieces.append(moved(parts[d], lambda c, f, d=d: (c, f ^ d)))
    usable = quality_both.astype(jnp.bfloat16)[None, :]
    blocks = []
    start = 0
    for size in chunks:
        rows = slice(start * 2 * nb, (start + size) * 2 * nb)
        own = jnp.stack([x[rows] * usable for x in pieces])
        blocks.append(
            (own, moved(own, lambda c, f: (c + 2, f)), moved(own, lambda c, f: (c - 2, f)))
        )
        start += size
    results = []
    for k, (own, prev, nxt) in enumerate(blocks):
        far_type = jnp.bfloat16 if k == len(blocks) - 1 else jnp.float32
        if k:
            own, results[-4] = lax.optimization_barrier((own, results[-4]))
        mine, theirs, far_mine, far_theirs = cross(
            own, prev, nxt, reach_own, reach_prev, far_type
        )
        if k:
            tied = lax.optimization_barrier((theirs, far_mine, far_theirs, *results[-3:]))
            theirs, far_mine, far_theirs = tied[:3]
            results[-3:] = tied[3:]
        results += [
            mine,
            moved(theirs, lambda c, f: (c ^ 1, f)),
            moved(far_mine, lambda c, f: (c - 2, f)),
            moved(far_theirs, lambda c, f: ((c ^ 1) - 2, f)),
        ]
    return finish(count[None, :], results, count_a, half)[None]


def solution(mesh):
    return jax.shard_map(
        on_device,
        mesh=mesh,
        in_specs=(P("chan", "freq"), P(), P()),
        out_specs=P("chan", None, "freq", None),
        check_vma=False,
    )
```

```python
import functools
import math

import jax
import jax.numpy as jnp
import ml_dtypes
import numpy as np
from jax import lax
from jax.experimental import pallas as pl
from jax.experimental.pallas import tpu as pltpu
from jax.sharding import PartitionSpec as P

BAND = 256
TBLK = 128

band_low = 0.004
band_high = 0.48
level_eps = 1e-05
MIB = 1 << 20


def tap_values(offset, half_span):
    window = 0.5 + 0.5 * np.cos(np.pi * offset / (half_span + 1))
    response = 2.0 * band_high * np.sinc(2.0 * band_high * offset) - 2.0 * band_low * np.sinc(
        2.0 * band_low * offset
    )
    return np.where(np.abs(offset) <= half_span, window * response, 0.0)


def stencil_table(boxed):
    offset = np.arange(2 * TBLK)[None, :] + TBLK - np.arange(4 * TBLK)[:, None]
    if boxed:
        values = np.where(np.abs(offset) <= TBLK, 1.0, 0.0)
    else:
        values = tap_values(offset.astype(np.float64), TBLK)
    return values.astype(ml_dtypes.bfloat16)


def dft_tables(count_a, n_freq):
    pad_a = -(-count_a // 16) * 16
    length = count_a * TBLK
    index = np.arange(count_a)
    angle = (index[:, None] * index[None, :] % count_a) * (2.0 * np.pi / count_a)
    first = np.zeros((2, pad_a, pad_a))
    first[0, :count_a, :count_a] = np.cos(angle)
    first[1, :count_a, :count_a] = -np.sin(angle)
    first = first.reshape(2 * pad_a, pad_a).astype(ml_dtypes.bfloat16)
    twist = np.zeros((2, pad_a, TBLK), np.float32)
    turn = (index[:, None] * np.arange(TBLK)[None, :] % length) * (2.0 * np.pi / length)
    twist[0, :count_a] = np.cos(turn)
    twist[1, :count_a] = np.sin(turn)
    k2_count = TBLK // 2
    turn = (np.arange(k2_count)[:, None] * np.arange(TBLK)[None, :] % TBLK) * (2.0 * np.pi / TBLK)
    real = np.concatenate([np.cos(turn), np.sin(turn)], axis=1)
    imag = np.concatenate([-np.sin(turn), np.cos(turn)], axis=1)
    half = k2_count // n_freq // 2
    second = np.stack([real, imag]).reshape(2, n_freq, 2, half, 2 * TBLK)
    second = second.transpose(1, 2, 0, 3, 4).reshape(n_freq, 2, 2 * half, 2 * TBLK)
    return first, twist, second.astype(ml_dtypes.bfloat16)


def block_bins(n_freq):
    return 16 if n_freq <= 4 else 8


def whole(shape):
    return pl.BlockSpec(shape, lambda t: (0,) * len(shape))


def spectra_kernel(
    count_a,
    n_freq,
    chunks,
    own,
    other,
    near_own,
    near_other,
    off_own,
    off_other,
    taps,
    box,
    first,
    twist,
    second,
    *rest,
):
    outs = rest[: n_freq * len(chunks)]
    padded, filtered, magnitude, whitened, tw_re, tw_im = rest[len(outs) :]
    core, band = lax.axis_index("chan") % 2, lax.axis_index("freq")
    ch = own.shape[0]
    both = 2 * ch
    pad_a = first.shape[1]
    dot = functools.partial(jnp.dot, preferred_element_type=jnp.float32)

    even = band % 2 == 0
    sides = ((own, near_own, off_own), (other, near_other, off_other))
    for which, (mid, near, off) in enumerate(sides):
        near, off = near[...], off[...]
        lo, hi = jnp.where(even, off, near), jnp.where(even, near, off)
        lo = jnp.where(band > 0, lo, jnp.zeros_like(lo))
        hi = jnp.where(band < n_freq - 1, hi, jnp.zeros_like(hi))
        base = core if which == 0 else 1 - core
        rows = pl.ds(pl.multiple_of(base * ch, ch), ch)
        for j in range(2):
            padded[j, rows, :] = lo[:, j * TBLK : (j + 1) * TBLK]
            padded[count_a + 2 + j, rows, :] = hi[:, j * TBLK : (j + 1) * TBLK]
        for j in range(count_a):
            padded[2 + j, rows, :] = mid[:, j * TBLK : (j + 1) * TBLK]

    def fir(i, carry):
        j = 2 * i
        window = jnp.concatenate([padded[j + n] for n in range(4)], axis=1)
        result = dot(window, taps[...])
        for n in range(2):
            part = result[:, n * TBLK : (n + 1) * TBLK]
            filtered[j + n] = part
            magnitude[j + n] = jnp.abs(part).astype(jnp.bfloat16)
        return carry

    lax.fori_loop(0, count_a // 2 + 1, fir, 0, unroll=True)

    def whiten(i, carry):
        j = 2 * i
        window = jnp.concatenate([magnitude[j + n] for n in range(4)], axis=1)
        level = dot(window, box[...]) / (2 * TBLK + 1)
        for n in range(2):
            part = filtered[j + n + 1] / (level[:, n * TBLK : (n + 1) * TBLK] + level_eps)
            rows = pl.ds(pl.multiple_of((j + n) * both, both), both)
            whitened[rows, :] = part
        return carry

    lax.fori_loop(0, count_a // 2, whiten, 0, unroll=True)
    whitened[count_a * both : pad_a * both, :] = jnp.zeros(
        ((pad_a - count_a) * both, TBLK), jnp.float32
    )

    def sections(i, carry):
        c = 2 * i
        pair = [
            whitened[pl.ds(c + n, pad_a, stride=both), :].astype(jnp.bfloat16) for n in range(2)
        ]
        section = dot(first[...], jnp.concatenate(pair, axis=1))
        for n in range(2):
            re = section[:pad_a, n * TBLK : (n + 1) * TBLK]
            im = section[pad_a:, n * TBLK : (n + 1) * TBLK]
            rows = pl.ds(pl.multiple_of((c + n) * pad_a, pad_a), pad_a)
            tw_re[rows, :] = re * twist[0] + im * twist[1]
            tw_im[rows, :] = im * twist[0] - re * twist[1]
        return carry

    lax.fori_loop(0, both // 2, sections, 0, unroll=True)

    rk = second.shape[2]
    half = rk // 2
    group = block_bins(n_freq) // half
    scale = 1.0 / math.sqrt(count_a * TBLK)
    turn = jnp.concatenate([second[band ^ d, core] for d in range(n_freq)], axis=0)

    def bins(k, start, i):
        results = []
        for n in range(group):
            k1 = (start + i) * group + n
            re = tw_re[pl.ds(k1, both, stride=pad_a), :].astype(jnp.bfloat16)
            im = tw_im[pl.ds(k1, both, stride=pad_a), :].astype(jnp.bfloat16)
            result = lax.dot_general(
                turn,
                jnp.concatenate([re, im], axis=1),
                (((1,), (1,)), ((), ())),
                preferred_element_type=jnp.float32,
            )
            results.append(result * scale)
        rows = pl.ds(i * group * rk, group * rk)
        for d in range(n_freq):
            starts = [d * rk + p * half for p in range(2)]
            block = jnp.concatenate([r[s : s + half] for s in starts for r in results], axis=0)
            outs[k * n_freq + d][rows, :] = block.astype(jnp.bfloat16)

    start = 0
    for k, size in enumerate(chunks):
        for i in range(size):
            bins(k, start, i)
        start += size


def spectra(own, other, halos, n_freq, chunks):
    ch, length = own.shape
    count_a = length // TBLK
    first, twist, second = dft_tables(count_a, n_freq)
    rk = second.shape[2]
    pad_a = first.shape[1]
    both = 2 * ch
    rows = 2 * block_bins(n_freq)
    shapes = [(size * rows, both) for size in chunks for _ in range(n_freq)]
    tables = (stencil_table(False), stencil_table(True), first, twist, second)
    operands = (own, other, *halos, *(jnp.asarray(t) for t in tables))
    return pl.pallas_call(
        functools.partial(spectra_kernel, count_a, n_freq, chunks),
        grid=(1,),
        out_shape=[jax.ShapeDtypeStruct(shape, jnp.bfloat16) for shape in shapes],
        in_specs=[whole(x.shape) for x in operands],
        out_specs=[whole(shape) for shape in shapes],
        scratch_shapes=[
            pltpu.VMEM((count_a + 4, both, TBLK), jnp.bfloat16),
            pltpu.VMEM((count_a + 2, both, TBLK), jnp.float32),
            pltpu.VMEM((count_a + 2, both, TBLK), jnp.bfloat16),
            pltpu.VMEM((pad_a * both, TBLK), jnp.float32),
            pltpu.VMEM((both * pad_a, TBLK), jnp.float32),
            pltpu.VMEM((both * pad_a, TBLK), jnp.float32),
        ],
        compiler_params=pltpu.CompilerParams(vmem_limit_bytes=62 * MIB),
        cost_estimate=pl.CostEstimate(
            flops=6 * 10**9, bytes_accessed=4 * 10**6, transcendentals=0
        ),
        name="spectra",
    )(*operands)


def cross_kernel(
    per,
    reach_own,
    reach_prev,
    turn_ref,
    pick_ref,
    cut_ref,
    own_ref,
    near_chip_ref,
    off_chip_ref,
    mine_ref,
    theirs_ref,
    far_mine_ref,
    far_theirs_ref,
    w_near,
    w_far,
    edge,
    sum_one,
    sum_two,
    sum_far,
):
    step = pl.program_id(0)
    n_seg, rb, both = own_ref.shape
    rb //= per
    depth = turn_ref.shape[0]
    nb = pick_ref.shape[0]
    slabs = both // 8
    me = lax.axis_index("chan")
    first_core = me % 2 == 0
    chip = me // 2
    last_chip = lax.axis_size("chan") // 2 - 1

    def beside(j):
        rows = slice(j * rb, (j + 1) * rb)
        near, off = near_chip_ref[:, rows, :], off_chip_ref[:, rows, :]
        even = chip % 2 == 0
        prev, nxt = jnp.where(even, off, near), jnp.where(even, near, off)
        prev = jnp.where(chip > 0, prev, jnp.zeros_like(prev))
        nxt = jnp.where(chip < last_chip, nxt, jnp.zeros_like(nxt))
        return prev, nxt

    @pl.when(step == 0)
    def _():
        row = lax.broadcasted_iota(jnp.int32, (16, both), 0) % 8
        col = lax.broadcasted_iota(jnp.int32, (16, both), 1)
        offset = (both + col - row).astype(jnp.float32)
        columns = [
            jnp.broadcast_to(r[...], (both, both)).T for r in (reach_own, reach_prev)
        ]
        wide = jnp.concatenate([columns[1], columns[1]], axis=1)
        for a in range(slabs):
            mine = columns[0][a * 8 : a * 8 + 8]
            lent = columns[1][a * 8 : a * 8 + 8]
            mine = jnp.concatenate([mine, mine], axis=0)
            lent = jnp.concatenate([lent, lent], axis=0)
            inner = col < both - 8 * a
            w_near[a] = jnp.where(inner & ((col < row) | (offset < mine)), 1.0, 0.0)
            w_far[a] = jnp.where(~inner & (offset < lent), 1.0, 0.0)
        row = lax.broadcasted_iota(jnp.int32, (both, 2 * both), 0)
        col = lax.broadcasted_iota(jnp.int32, (both, 2 * both), 1)
        same = (row // (both // 2)) == (col // both)
        for d in range(1, 8):
            hit = same & (col % both == both - d) & (row % 8 >= d)
            hit = hit & (2 * both - d < wide)
            edge[(d - 1) * both : d * both, :] = jnp.where(hit, 1.0, 0.0).astype(jnp.bfloat16)

    def left_rows(block):
        re = block.astype(jnp.float32).T.astype(jnp.bfloat16)
        im = jnp.dot(re, turn_ref[...], preferred_element_type=jnp.float32)
        re = re.astype(jnp.float32).reshape(slabs, 8, depth)
        im = im.reshape(slabs, 8, depth)
        return jnp.stack([re, im], axis=1).reshape(slabs, 16, depth).astype(jnp.bfloat16)

    def dots(j):
        own = own_ref[:, j * rb : (j + 1) * rb, :].reshape(depth, both)
        prev, nxt = (x.reshape(depth, both) for x in beside(j))
        left = jnp.concatenate([left_rows(own), left_rows(prev)], axis=2)
        pick = pick_ref[...]

        zero = jnp.zeros_like(own)
        for a in range(slabs):
            g, first = divmod(a, slabs // 2)
            if a == 0:
                right = jnp.concatenate(
                    [jnp.concatenate([own, nxt], axis=1), jnp.concatenate([zero, zero], axis=1)],
                    axis=0,
                )
            else:
                moved_own = pltpu.roll(own, both - 8 * a, 1).reshape(depth // 16, 16, both)
                moved_next = pltpu.roll(nxt, both - 8 * a, 1).reshape(depth // 16, 16, both)
                cut = cut_ref[a][None]
                inner = moved_next * cut
                outer = moved_next - inner
                local = (moved_own * cut + outer).reshape(depth, both)
                inner = inner.reshape(depth, both)
                outer = outer.reshape(depth, both)
                right = jnp.concatenate(
                    [
                        jnp.concatenate([local, inner], axis=1),
                        jnp.concatenate([zero, outer], axis=1),
                    ],
                    axis=0,
                )
            rows = (left[a][None] * pick).reshape(nb * 16, 2 * depth)
            result = jnp.dot(rows, right, preferred_element_type=jnp.float32)
            one = result[:, :both]
            two = result[:, both:].reshape(nb, 16, both)
            near = (two * w_near[a][None]).reshape(nb * 16, both)
            far = (two * w_far[a][None]).reshape(nb * 16, both)
            if first == 0:
                sum_one[2 * j + g], sum_two[2 * j + g], sum_far[2 * j + g] = one, near, far
            else:
                sum_one[2 * j + g] += one
                sum_two[2 * j + g] += near
                sum_far[2 * j + g] += far


    def margins(j):
        def split(x):
            return x[:nb], x[nb:]

        prev, nxt = (x.astype(jnp.float32) for x in beside(j))
        lefts = [split(prev[s]) for s in range(n_seg)]
        rights = [split(nxt[s]) for s in range(n_seg)]
        pieces = []
        for d in range(1, 8):
            re = im = None
            for (xr, xi), (yr, yi) in zip(lefts, rights):
                yr, yi = pltpu.roll(yr, d, 1), pltpu.roll(yi, d, 1)
                r, i = xr * yr + xi * yi, xi * yr - xr * yi
                re, im = (r, i) if re is None else (re + r, im + i)
            pieces.append(jnp.concatenate([re, im], axis=0).astype(jnp.bfloat16))
        margin = jnp.dot(
            jnp.concatenate(pieces, axis=1), edge[...], preferred_element_type=jnp.float32
        )


        return margin

    def diag(j, margin):
        lane = lax.broadcasted_iota(jnp.int32, (nb, both), 1)
        for p in range(2):
            values = []
            for g in range(2):
                low = high = far = None
                for b in range(8):
                    rows = pl.ds(p * 8 + b, nb, stride=16)
                    one, two, three = sum_one[2 * j + g, rows, :], sum_two[2 * j + g, rows, :], sum_far[2 * j + g, rows, :]
                    if b == 0:
                        low, high, far = one, two, three
                        continue
                    low += pltpu.roll(jnp.where(lane >= b, one, two), both - b, 1)
                    high += pltpu.roll(jnp.where(lane >= b, two, 0.0), both - b, 1)
                    far += pltpu.roll(three, both - b, 1)
                far += margin[p * nb : (p + 1) * nb, g * both : (g + 1) * both]
                values.append((low, high, far))
            mine = [jnp.where(first_core, x, y) for x, y in zip(*values)]
            theirs = [jnp.where(first_core, y, x) for x, y in zip(*values)]
            for near_ref, far_ref, value in (
                (mine_ref, far_mine_ref, mine),
                (theirs_ref, far_theirs_ref, theirs),
            ):
                near_ref[p, j, :nb] = value[0]
                near_ref[p, j, nb:] = value[1]
                far_ref[p, j] = value[2].astype(far_ref.dtype)

    for j in range(per):
        dots(j)
    margin = [margins(j) for j in range(per)]
    for j in range(per):
        diag(j, margin[j])


def cross(own, near_chip, off_chip, reach_own, reach_prev, far_type):
    n_seg, rows, both = own.shape
    nb = block_bins(n_seg)
    rb = 2 * nb
    depth = n_seg * rb
    steps = rows // rb
    slabs = both // 8
    per = 2 if steps % 2 == 0 else 1
    lane = np.arange(depth)
    part = lane % rb // nb
    turn = np.zeros((depth, depth))
    turn[lane + np.where(part == 0, nb, -nb), lane] = np.where(part == 0, 1.0, -1.0)
    lane = np.arange(2 * depth)
    pick = (lane % nb == np.arange(nb)[:, None, None]).astype(np.float32)
    pick = np.broadcast_to(pick, (nb, 16, 2 * depth))
    cut = np.arange(both) < both - 8 * np.arange(slabs)[:, None, None]
    cut = np.broadcast_to(cut, (slabs, 16, both))
    tables = [jnp.asarray(x.astype(ml_dtypes.bfloat16)) for x in (turn, pick, cut)]
    fixed = (reach_own, reach_prev, *tables)
    near = jax.ShapeDtypeStruct((2, steps, 2 * nb, both), jnp.float32)
    far = jax.ShapeDtypeStruct((2, steps, nb, both), far_type)
    near_spec = pl.BlockSpec((2, per, 2 * nb, both), lambda t: (0, t, 0, 0))
    far_spec = pl.BlockSpec((2, per, nb, both), lambda t: (0, t, 0, 0))
    block = pl.BlockSpec((n_seg, per * rb, both), lambda t: (0, t, 0))
    return pl.pallas_call(
        functools.partial(cross_kernel, per),
        grid=(steps // per,),
        out_shape=[near, near, far, far],
        in_specs=[whole(x.shape) for x in fixed] + [block] * 3,
        out_specs=[near_spec, near_spec, far_spec, far_spec],
        scratch_shapes=[
            pltpu.VMEM((slabs, 16, both), jnp.float32),
            pltpu.VMEM((slabs, 16, both), jnp.float32),
            pltpu.VMEM((7 * both, 2 * both), jnp.bfloat16),
            pltpu.VMEM((2 * per, nb * 16, both), jnp.float32),
            pltpu.VMEM((2 * per, nb * 16, both), jnp.float32),
            pltpu.VMEM((2 * per, nb * 16, both), jnp.float32),
        ],
        compiler_params=pltpu.CompilerParams(
            dimension_semantics=("arbitrary",), vmem_limit_bytes=24 * MIB
        ),
        cost_estimate=pl.CostEstimate(
            flops=10**9 * steps, bytes_accessed=2 * 10**5 * steps, transcendentals=0
        ),
        name="cross",
    )(*fixed, own, near_chip, off_chip)


def finish_kernel(count_a, half, chunks, count, *rest):
    parts, out_ref, stage = rest[: 4 * chunks], rest[4 * chunks], rest[4 * chunks + 1]
    core = lax.axis_index("chan") % 2
    bins = out_ref.shape[1] // 2
    inverse = 1.0 / count[...]
    k1 = 0
    for chunk in range(chunks):
        mine, theirs, far_mine, far_theirs = parts[4 * chunk : 4 * chunk + 4]
        steps, nb, both = far_mine.shape[1:]
        for t in range(steps):
            for which, (near, far) in enumerate(((mine, far_mine), (theirs, far_theirs))):
                base = (core if which == 0 else 1 - core) * bins
                value = near[0, t]
                low = value[:nb] * inverse[:, :both]
                high = (value[nb:] + far[0, t].astype(jnp.float32)) * inverse[:, both:]
                for r, x in enumerate((low, high)):
                    for n in range(nb // half):
                        place = pl.ds(base + k1 + n, half, stride=count_a)
                        stage[r, place, :] = x[n * half : (n + 1) * half]
            k1 += nb // half
    for r in range(2):
        both = stage.shape[2]
        out_ref[0, :, r * both : (r + 1) * both] = stage[r]


def finish(count, parts, count_a, half):
    bins = count_a * half

    def half_of(shape):
        return pl.BlockSpec((1,) + shape[1:], lambda p: (p,) + (0,) * (len(shape) - 1))

    return pl.pallas_call(
        functools.partial(finish_kernel, count_a, half, len(parts) // 4),
        grid=(2,),
        out_shape=jax.ShapeDtypeStruct((2, 2 * bins, BAND), jnp.float32),
        in_specs=[whole(count.shape)] + [half_of(x.shape) for x in parts],
        out_specs=half_of((2, 2 * bins, BAND)),
        scratch_shapes=[pltpu.VMEM((2, 2 * bins, TBLK), jnp.float32)],
        compiler_params=pltpu.CompilerParams(vmem_limit_bytes=24 * MIB),
        name="finish",
    )(count, *parts)


def skew_rows(matrix, keep):
    height, width = matrix.shape
    flat = jnp.pad(matrix.reshape(height * width), (0, height))
    return flat.reshape(height, width + 1)[:, :keep]


def pair_count(quality_ext, reach_own, band):
    channel_count = reach_own.shape[0]
    ext_len = quality_ext.shape[0]
    partner = skew_rows(jnp.broadcast_to(quality_ext[None, :], (channel_count, ext_len)), band)
    offsets = jnp.arange(band, dtype=jnp.int32)[None, :]
    inside = (offsets < reach_own[:, None]).astype(jnp.int32)
    weight = quality_ext[:channel_count, None] * partner * inside
    return jnp.maximum(jnp.sum(weight.astype(jnp.float32), axis=0), 1.0)


def on_device(strain, quality, offset_reach):
    ch, length = strain.shape
    both = 2 * ch
    assert both == TBLK and BAND == 2 * both
    n_chan, n_freq = lax.axis_size("chan"), lax.axis_size("freq")
    count_a = length // TBLK
    rk = TBLK // 2 // n_freq
    me = lax.axis_index("chan")
    chip = me // 2

    def moved(x, target):
        pairs = []
        for c in range(n_chan):
            for f in range(n_freq):
                to = target(c, f)
                if 0 <= to[0] < n_chan and 0 <= to[1] < n_freq:
                    pairs.append((c * n_freq + f, to[0] * n_freq + to[1]))
        return lax.ppermute(x, ("chan", "freq"), pairs)

    def paired(at, count, off):
        to = ((at + off) ^ 1) - off
        return to if 0 <= to < count else at

    tail, head = strain[:, length - 2 * TBLK :], strain[:, : 2 * TBLK]
    even = lax.axis_index("freq") % 2 == 0
    ends = (jnp.where(even, tail, head), jnp.where(even, head, tail))
    other = moved(strain, lambda c, f: (c ^ 1, f))
    halos = [
        moved(ends[off], lambda c, f, o=off, k=flip: (c ^ k, paired(f, n_freq, o)))
        for off in range(2)
        for flip in range(2)
    ]

    quality_pad = jnp.pad(quality, (0, BAND + both))
    reach_pad = jnp.pad(offset_reach, (both, 0))
    quality_both = lax.dynamic_slice_in_dim(quality_pad, chip * both, both, 0)
    reach_pad = reach_pad.astype(jnp.float32)
    reach_own = lax.dynamic_slice_in_dim(reach_pad, (chip + 1) * both, both, 0)[None, :]
    reach_prev = lax.dynamic_slice_in_dim(reach_pad, chip * both, both, 0)[None, :]
    quality_ext = lax.dynamic_slice_in_dim(quality_pad, me * ch, ch + BAND, 0)
    count = pair_count(quality_ext, lax.dynamic_slice_in_dim(offset_reach, me * ch, ch, 0), BAND)

    half = rk // 2
    nb = block_bins(n_freq)
    steps = count_a * half // nb
    first = steps // 3
    chunks = (first, steps - first)
    parts = spectra(strain, other, halos, n_freq, chunks)
    usable = quality_both.astype(jnp.bfloat16)[None, :]
    blocks = []
    for k in range(len(chunks)):
        pieces = list(parts[k * n_freq : (k + 1) * n_freq])
        for d in range(1, n_freq):
            pieces[d] = moved(pieces[d], lambda c, f, d=d: (c, f ^ d))
        own = jnp.stack([x * usable for x in pieces])
        blocks.append(
            [own]
            + [
                moved(own, lambda c, f, o=off: (2 * paired(c // 2, n_chan // 2, o) + c % 2, f))
                for off in range(2)
            ]
        )
    results = []
    for k, (own, near_chip, off_chip) in enumerate(blocks):
        far_type = jnp.bfloat16 if k == len(blocks) - 1 else jnp.float32
        if k:
            own, results[-4] = lax.optimization_barrier((own, results[-4]))
        mine, theirs, far_mine, far_theirs = cross(
            own, near_chip, off_chip, reach_own, reach_prev, far_type
        )
        if k:
            tied = lax.optimization_barrier((theirs, far_mine, far_theirs, *results[-3:]))
            theirs, far_mine, far_theirs = tied[:3]
            results[-3:] = tied[3:]
        results += [
            mine,
            moved(theirs, lambda c, f: (c ^ 1, f)),
            moved(far_mine, lambda c, f: (c - 2, f)),
            moved(far_theirs, lambda c, f: ((c ^ 1) - 2, f)),
        ]
    return finish(count[None, :], results, count_a, half)[None]


def solution(mesh):
    return jax.shard_map(
        on_device,
        mesh=mesh,
        in_specs=(P("chan", "freq"), P(), P()),
        out_specs=P("chan", None, "freq", None),
        check_vma=False,
    )
```

```python
import functools
import math

import jax
import jax.numpy as jnp
import ml_dtypes
import numpy as np
from jax import lax
from jax.experimental import pallas as pl
from jax.experimental.pallas import tpu as pltpu
from jax.sharding import PartitionSpec as P

BAND = 256
TBLK = 128

band_low = 0.004
band_high = 0.48
level_eps = 1e-05
MIB = 1 << 20


def tap_values(offset, half_span):
    window = 0.5 + 0.5 * np.cos(np.pi * offset / (half_span + 1))
    response = 2.0 * band_high * np.sinc(2.0 * band_high * offset) - 2.0 * band_low * np.sinc(
        2.0 * band_low * offset
    )
    return np.where(np.abs(offset) <= half_span, window * response, 0.0)


def stencil_table(boxed):
    offset = np.arange(2 * TBLK)[None, :] + TBLK - np.arange(4 * TBLK)[:, None]
    if boxed:
        values = np.where(np.abs(offset) <= TBLK, 1.0, 0.0)
    else:
        values = tap_values(offset.astype(np.float64), TBLK)
    return values.astype(ml_dtypes.bfloat16)


def dft_tables(count_a, n_freq):
    pad_a = -(-count_a // 16) * 16
    length = count_a * TBLK
    index = np.arange(count_a)
    angle = (index[:, None] * index[None, :] % count_a) * (2.0 * np.pi / count_a)
    first = np.zeros((2, pad_a, pad_a))
    first[0, :count_a, :count_a] = np.cos(angle)
    first[1, :count_a, :count_a] = -np.sin(angle)
    first = first.reshape(2 * pad_a, pad_a).astype(ml_dtypes.bfloat16)
    twist = np.zeros((2, pad_a, TBLK), np.float32)
    turn = (index[:, None] * np.arange(TBLK)[None, :] % length) * (2.0 * np.pi / length)
    twist[0, :count_a] = np.cos(turn)
    twist[1, :count_a] = np.sin(turn)
    k2_count = TBLK // 2
    turn = (np.arange(k2_count)[:, None] * np.arange(TBLK)[None, :] % TBLK) * (2.0 * np.pi / TBLK)
    real = np.concatenate([np.cos(turn), np.sin(turn)], axis=1)
    imag = np.concatenate([-np.sin(turn), np.cos(turn)], axis=1)
    half = k2_count // n_freq // 2
    second = np.stack([real, imag]).reshape(2, n_freq, 2, half, 2 * TBLK)
    second = second.transpose(1, 2, 0, 3, 4).reshape(n_freq, 2, 2 * half, 2 * TBLK)
    return first, twist, second.astype(ml_dtypes.bfloat16)


def block_bins(n_freq):
    return 16 if n_freq <= 4 else 8


def whole(shape):
    return pl.BlockSpec(shape, lambda t: (0,) * len(shape))


def spectra_kernel(
    count_a,
    n_freq,
    chunks,
    own,
    other,
    near_own,
    near_other,
    off_own,
    off_other,
    taps,
    box,
    first,
    twist,
    second,
    *rest,
):
    outs = rest[: n_freq * len(chunks)]
    padded, filtered, magnitude, whitened, tw_re, tw_im = rest[len(outs) :]
    core, band = lax.axis_index("chan") % 2, lax.axis_index("freq")
    ch = own.shape[0]
    both = 2 * ch
    pad_a = first.shape[1]
    dot = functools.partial(jnp.dot, preferred_element_type=jnp.float32)

    even = band % 2 == 0
    sides = ((own, near_own, off_own), (other, near_other, off_other))
    for which, (mid, near, off) in enumerate(sides):
        near, off = near[...], off[...]
        lo, hi = jnp.where(even, off, near), jnp.where(even, near, off)
        lo = jnp.where(band > 0, lo, jnp.zeros_like(lo))
        hi = jnp.where(band < n_freq - 1, hi, jnp.zeros_like(hi))
        base = core if which == 0 else 1 - core
        rows = pl.ds(pl.multiple_of(base * ch, ch), ch)
        for j in range(2):
            padded[j, rows, :] = lo[:, j * TBLK : (j + 1) * TBLK]
            padded[count_a + 2 + j, rows, :] = hi[:, j * TBLK : (j + 1) * TBLK]
        for j in range(count_a):
            padded[2 + j, rows, :] = mid[:, j * TBLK : (j + 1) * TBLK]

    def fir(i, carry):
        j = 2 * i
        window = jnp.concatenate([padded[j + n] for n in range(4)], axis=1)
        result = dot(window, taps[...])
        for n in range(2):
            part = result[:, n * TBLK : (n + 1) * TBLK]
            filtered[j + n] = part
            magnitude[j + n] = jnp.abs(part).astype(jnp.bfloat16)
        return carry

    lax.fori_loop(0, count_a // 2 + 1, fir, 0, unroll=True)

    def whiten(i, carry):
        j = 2 * i
        window = jnp.concatenate([magnitude[j + n] for n in range(4)], axis=1)
        level = dot(window, box[...]) / (2 * TBLK + 1)
        for n in range(2):
            part = filtered[j + n + 1] / (level[:, n * TBLK : (n + 1) * TBLK] + level_eps)
            rows = pl.ds(pl.multiple_of((j + n) * both, both), both)
            whitened[rows, :] = part
        return carry

    lax.fori_loop(0, count_a // 2, whiten, 0, unroll=True)
    whitened[count_a * both : pad_a * both, :] = jnp.zeros(
        ((pad_a - count_a) * both, TBLK), jnp.float32
    )

    def sections(i, carry):
        c = 2 * i
        pair = [
            whitened[pl.ds(c + n, pad_a, stride=both), :].astype(jnp.bfloat16) for n in range(2)
        ]
        section = dot(first[...], jnp.concatenate(pair, axis=1))
        for n in range(2):
            re = section[:pad_a, n * TBLK : (n + 1) * TBLK]
            im = section[pad_a:, n * TBLK : (n + 1) * TBLK]
            rows = pl.ds(pl.multiple_of((c + n) * pad_a, pad_a), pad_a)
            tw_re[rows, :] = re * twist[0] + im * twist[1]
            tw_im[rows, :] = im * twist[0] - re * twist[1]
        return carry

    lax.fori_loop(0, both // 2, sections, 0, unroll=True)

    rk = second.shape[2]
    half = rk // 2
    group = block_bins(n_freq) // half
    scale = 1.0 / math.sqrt(count_a * TBLK)
    turn = jnp.concatenate([second[band ^ d, core] for d in range(n_freq)], axis=0)

    def bins(k, start, i):
        results = []
        for n in range(group):
            k1 = (start + i) * group + n
            re = tw_re[pl.ds(k1, both, stride=pad_a), :].astype(jnp.bfloat16)
            im = tw_im[pl.ds(k1, both, stride=pad_a), :].astype(jnp.bfloat16)
            result = lax.dot_general(
                turn,
                jnp.concatenate([re, im], axis=1),
                (((1,), (1,)), ((), ())),
                preferred_element_type=jnp.float32,
            )
            results.append(result * scale)
        rows = pl.ds(i * group * rk, group * rk)
        for d in range(n_freq):
            starts = [d * rk + p * half for p in range(2)]
            block = jnp.concatenate([r[s : s + half] for s in starts for r in results], axis=0)
            outs[k * n_freq + d][rows, :] = block.astype(jnp.bfloat16)

    start = 0
    for k, size in enumerate(chunks):
        for i in range(size):
            bins(k, start, i)
        start += size


def spectra(own, other, halos, n_freq, chunks):
    ch, length = own.shape
    count_a = length // TBLK
    first, twist, second = dft_tables(count_a, n_freq)
    rk = second.shape[2]
    pad_a = first.shape[1]
    both = 2 * ch
    rows = 2 * block_bins(n_freq)
    shapes = [(size * rows, both) for size in chunks for _ in range(n_freq)]
    tables = (stencil_table(False), stencil_table(True), first, twist, second)
    operands = (own, other, *halos, *(jnp.asarray(t) for t in tables))
    return pl.pallas_call(
        functools.partial(spectra_kernel, count_a, n_freq, chunks),
        grid=(1,),
        out_shape=[jax.ShapeDtypeStruct(shape, jnp.bfloat16) for shape in shapes],
        in_specs=[whole(x.shape) for x in operands],
        out_specs=[whole(shape) for shape in shapes],
        scratch_shapes=[
            pltpu.VMEM((count_a + 4, both, TBLK), jnp.bfloat16),
            pltpu.VMEM((count_a + 2, both, TBLK), jnp.float32),
            pltpu.VMEM((count_a + 2, both, TBLK), jnp.bfloat16),
            pltpu.VMEM((pad_a * both, TBLK), jnp.float32),
            pltpu.VMEM((both * pad_a, TBLK), jnp.float32),
            pltpu.VMEM((both * pad_a, TBLK), jnp.float32),
        ],
        compiler_params=pltpu.CompilerParams(vmem_limit_bytes=62 * MIB),
        cost_estimate=pl.CostEstimate(
            flops=6 * 10**9, bytes_accessed=4 * 10**6, transcendentals=0
        ),
        name="spectra",
    )(*operands)


def cross_kernel(
    per,
    reach_own,
    reach_prev,
    turn_ref,
    pick_ref,
    cut_ref,
    own_ref,
    near_chip_ref,
    off_chip_ref,
    mine_ref,
    theirs_ref,
    far_mine_ref,
    far_theirs_ref,
    w_near,
    w_far,
    edge,
    sum_one,
    sum_two,
    sum_far,
):
    step = pl.program_id(0)
    n_seg, rb, both = own_ref.shape
    rb //= per
    depth = turn_ref.shape[0]
    nb = pick_ref.shape[0]
    slabs = both // 8
    me = lax.axis_index("chan")
    first_core = me % 2 == 0
    chip = me // 2
    last_chip = lax.axis_size("chan") // 2 - 1

    def beside(j):
        rows = slice(j * rb, (j + 1) * rb)
        near, off = near_chip_ref[:, rows, :], off_chip_ref[:, rows, :]
        even = chip % 2 == 0
        prev, nxt = jnp.where(even, off, near), jnp.where(even, near, off)
        prev = jnp.where(chip > 0, prev, jnp.zeros_like(prev))
        nxt = jnp.where(chip < last_chip, nxt, jnp.zeros_like(nxt))
        return prev, nxt

    @pl.when(step == 0)
    def _():
        row = lax.broadcasted_iota(jnp.int32, (16, both), 0) % 8
        col = lax.broadcasted_iota(jnp.int32, (16, both), 1)
        offset = (both + col - row).astype(jnp.float32)
        columns = [
            jnp.broadcast_to(r[...], (both, both)).T for r in (reach_own, reach_prev)
        ]
        wide = jnp.concatenate([columns[1], columns[1]], axis=1)
        for a in range(slabs):
            mine = columns[0][a * 8 : a * 8 + 8]
            lent = columns[1][a * 8 : a * 8 + 8]
            mine = jnp.concatenate([mine, mine], axis=0)
            lent = jnp.concatenate([lent, lent], axis=0)
            inner = col < both - 8 * a
            w_near[a] = jnp.where(inner & ((col < row) | (offset < mine)), 1.0, 0.0)
            w_far[a] = jnp.where(~inner & (offset < lent), 1.0, 0.0)
        row = lax.broadcasted_iota(jnp.int32, (both, 2 * both), 0)
        col = lax.broadcasted_iota(jnp.int32, (both, 2 * both), 1)
        same = (row // (both // 2)) == (col // both)
        for d in range(1, 8):
            hit = same & (col % both == both - d) & (row % 8 >= d)
            hit = hit & (2 * both - d < wide)
            edge[(d - 1) * both : d * both, :] = jnp.where(hit, 1.0, 0.0).astype(jnp.bfloat16)

    def left_rows(block):
        re = block.astype(jnp.float32).T.astype(jnp.bfloat16)
        im = jnp.dot(re, turn_ref[...], preferred_element_type=jnp.float32)
        re = re.astype(jnp.float32).reshape(slabs, 8, depth)
        im = im.reshape(slabs, 8, depth)
        return jnp.stack([re, im], axis=1).reshape(slabs, 16, depth).astype(jnp.bfloat16)

    def dots(j):
        own = own_ref[:, j * rb : (j + 1) * rb, :].reshape(depth, both)
        prev, nxt = (x.reshape(depth, both) for x in beside(j))
        left = jnp.concatenate([left_rows(own), left_rows(prev)], axis=2)
        pick = pick_ref[...]

        zero = jnp.zeros_like(own)
        for a in range(slabs):
            g, first = divmod(a, slabs // 2)
            if a == 0:
                right = jnp.concatenate(
                    [jnp.concatenate([own, nxt], axis=1), jnp.concatenate([zero, zero], axis=1)],
                    axis=0,
                )
            else:
                moved_own = pltpu.roll(own, both - 8 * a, 1).reshape(depth // 16, 16, both)
                moved_next = pltpu.roll(nxt, both - 8 * a, 1).reshape(depth // 16, 16, both)
                cut = cut_ref[a][None]
                inner = moved_next * cut
                outer = moved_next - inner
                local = (moved_own * cut + outer).reshape(depth, both)
                inner = inner.reshape(depth, both)
                outer = outer.reshape(depth, both)
                right = jnp.concatenate(
                    [
                        jnp.concatenate([local, inner], axis=1),
                        jnp.concatenate([zero, outer], axis=1),
                    ],
                    axis=0,
                )
            rows = (left[a][None] * pick).reshape(nb * 16, 2 * depth)
            result = jnp.dot(rows, right, preferred_element_type=jnp.float32)
            one = result[:, :both]
            two = result[:, both:].reshape(nb, 16, both)
            near = (two * w_near[a][None]).reshape(nb * 16, both)
            far = (two * w_far[a][None]).reshape(nb * 16, both)
            if first == 0:
                sum_one[2 * j + g], sum_two[2 * j + g], sum_far[2 * j + g] = one, near, far
            else:
                sum_one[2 * j + g] += one
                sum_two[2 * j + g] += near
                sum_far[2 * j + g] += far


    def margins(j):
        def split(x):
            return x[:nb], x[nb:]

        prev, nxt = (x.astype(jnp.float32) for x in beside(j))
        lefts = [split(prev[s]) for s in range(n_seg)]
        rights = [split(nxt[s]) for s in range(n_seg)]
        pieces = []
        for d in range(1, 8):
            re = im = None
            for (xr, xi), (yr, yi) in zip(lefts, rights):
                yr, yi = pltpu.roll(yr, d, 1), pltpu.roll(yi, d, 1)
                r, i = xr * yr + xi * yi, xi * yr - xr * yi
                re, im = (r, i) if re is None else (re + r, im + i)
            pieces.append(jnp.concatenate([re, im], axis=0).astype(jnp.bfloat16))
        margin = jnp.dot(
            jnp.concatenate(pieces, axis=1), edge[...], preferred_element_type=jnp.float32
        )


        return margin

    def diag(j, margin):
        lane = lax.broadcasted_iota(jnp.int32, (nb, both), 1)
        for p in range(2):
            values = []
            for g in range(2):
                low = high = far = None
                for b in range(8):
                    rows = pl.ds(p * 8 + b, nb, stride=16)
                    one, two, three = sum_one[2 * j + g, rows, :], sum_two[2 * j + g, rows, :], sum_far[2 * j + g, rows, :]
                    if b == 0:
                        low, high, far = one, two, three
                        continue
                    low += pltpu.roll(jnp.where(lane >= b, one, two), both - b, 1)
                    high += pltpu.roll(jnp.where(lane >= b, two, 0.0), both - b, 1)
                    far += pltpu.roll(three, both - b, 1)
                far += margin[p * nb : (p + 1) * nb, g * both : (g + 1) * both]
                values.append((low, high, far))
            mine = [jnp.where(first_core, x, y) for x, y in zip(*values)]
            theirs = [jnp.where(first_core, y, x) for x, y in zip(*values)]
            for near_ref, far_ref, value in (
                (mine_ref, far_mine_ref, mine),
                (theirs_ref, far_theirs_ref, theirs),
            ):
                near_ref[p, j, :nb] = value[0]
                near_ref[p, j, nb:] = value[1]
                far_ref[p, j] = value[2].astype(far_ref.dtype)

    for j in range(per):
        dots(j)
    margin = [margins(j) for j in range(per)]
    for j in range(per):
        diag(j, margin[j])


def cross(own, near_chip, off_chip, reach_own, reach_prev, far_type):
    n_seg, rows, both = own.shape
    nb = block_bins(n_seg)
    rb = 2 * nb
    depth = n_seg * rb
    steps = rows // rb
    slabs = both // 8
    per = max(n for n in (1, 2, 4) if steps % n == 0)
    lane = np.arange(depth)
    part = lane % rb // nb
    turn = np.zeros((depth, depth))
    turn[lane + np.where(part == 0, nb, -nb), lane] = np.where(part == 0, 1.0, -1.0)
    lane = np.arange(2 * depth)
    pick = (lane % nb == np.arange(nb)[:, None, None]).astype(np.float32)
    pick = np.broadcast_to(pick, (nb, 16, 2 * depth))
    cut = np.arange(both) < both - 8 * np.arange(slabs)[:, None, None]
    cut = np.broadcast_to(cut, (slabs, 16, both))
    tables = [jnp.asarray(x.astype(ml_dtypes.bfloat16)) for x in (turn, pick, cut)]
    fixed = (reach_own, reach_prev, *tables)
    near = jax.ShapeDtypeStruct((2, steps, 2 * nb, both), jnp.float32)
    far = jax.ShapeDtypeStruct((2, steps, nb, both), far_type)
    near_spec = pl.BlockSpec((2, per, 2 * nb, both), lambda t: (0, t, 0, 0))
    far_spec = pl.BlockSpec((2, per, nb, both), lambda t: (0, t, 0, 0))
    block = pl.BlockSpec((n_seg, per * rb, both), lambda t: (0, t, 0))
    return pl.pallas_call(
        functools.partial(cross_kernel, per),
        grid=(steps // per,),
        out_shape=[near, near, far, far],
        in_specs=[whole(x.shape) for x in fixed] + [block] * 3,
        out_specs=[near_spec, near_spec, far_spec, far_spec],
        scratch_shapes=[
            pltpu.VMEM((slabs, 16, both), jnp.float32),
            pltpu.VMEM((slabs, 16, both), jnp.float32),
            pltpu.VMEM((7 * both, 2 * both), jnp.bfloat16),
            pltpu.VMEM((2 * per, nb * 16, both), jnp.float32),
            pltpu.VMEM((2 * per, nb * 16, both), jnp.float32),
            pltpu.VMEM((2 * per, nb * 16, both), jnp.float32),
        ],
        compiler_params=pltpu.CompilerParams(
            dimension_semantics=("arbitrary",), vmem_limit_bytes=24 * MIB
        ),
        cost_estimate=pl.CostEstimate(
            flops=10**9 * steps, bytes_accessed=2 * 10**5 * steps, transcendentals=0
        ),
        name="cross",
    )(*fixed, own, near_chip, off_chip)


def finish_kernel(count_a, half, chunks, count, *rest):
    parts, out_ref, stage = rest[: 4 * chunks], rest[4 * chunks], rest[4 * chunks + 1]
    core = lax.axis_index("chan") % 2
    bins = out_ref.shape[1] // 2
    inverse = 1.0 / count[...]
    k1 = 0
    for chunk in range(chunks):
        mine, theirs, far_mine, far_theirs = parts[4 * chunk : 4 * chunk + 4]
        steps, nb, both = far_mine.shape[1:]
        for t in range(steps):
            for which, (near, far) in enumerate(((mine, far_mine), (theirs, far_theirs))):
                base = (core if which == 0 else 1 - core) * bins
                value = near[0, t]
                low = value[:nb] * inverse[:, :both]
                high = (value[nb:] + far[0, t].astype(jnp.float32)) * inverse[:, both:]
                for r, x in enumerate((low, high)):
                    for n in range(nb // half):
                        place = pl.ds(base + k1 + n, half, stride=count_a)
                        stage[r, place, :] = x[n * half : (n + 1) * half]
            k1 += nb // half
    for r in range(2):
        both = stage.shape[2]
        out_ref[0, :, r * both : (r + 1) * both] = stage[r]


def finish(count, parts, count_a, half):
    bins = count_a * half

    def half_of(shape):
        return pl.BlockSpec((1,) + shape[1:], lambda p: (p,) + (0,) * (len(shape) - 1))

    return pl.pallas_call(
        functools.partial(finish_kernel, count_a, half, len(parts) // 4),
        grid=(2,),
        out_shape=jax.ShapeDtypeStruct((2, 2 * bins, BAND), jnp.float32),
        in_specs=[whole(count.shape)] + [half_of(x.shape) for x in parts],
        out_specs=half_of((2, 2 * bins, BAND)),
        scratch_shapes=[pltpu.VMEM((2, 2 * bins, TBLK), jnp.float32)],
        compiler_params=pltpu.CompilerParams(vmem_limit_bytes=24 * MIB),
        name="finish",
    )(count, *parts)


def skew_rows(matrix, keep):
    height, width = matrix.shape
    flat = jnp.pad(matrix.reshape(height * width), (0, height))
    return flat.reshape(height, width + 1)[:, :keep]


def pair_count(quality_ext, reach_own, band):
    channel_count = reach_own.shape[0]
    ext_len = quality_ext.shape[0]
    partner = skew_rows(jnp.broadcast_to(quality_ext[None, :], (channel_count, ext_len)), band)
    offsets = jnp.arange(band, dtype=jnp.int32)[None, :]
    inside = (offsets < reach_own[:, None]).astype(jnp.int32)
    weight = quality_ext[:channel_count, None] * partner * inside
    return jnp.maximum(jnp.sum(weight.astype(jnp.float32), axis=0), 1.0)


def on_device(strain, quality, offset_reach):
    ch, length = strain.shape
    both = 2 * ch
    assert both == TBLK and BAND == 2 * both
    n_chan, n_freq = lax.axis_size("chan"), lax.axis_size("freq")
    count_a = length // TBLK
    rk = TBLK // 2 // n_freq
    me = lax.axis_index("chan")
    chip = me // 2

    def moved(x, target):
        pairs = []
        for c in range(n_chan):
            for f in range(n_freq):
                to = target(c, f)
                if 0 <= to[0] < n_chan and 0 <= to[1] < n_freq:
                    pairs.append((c * n_freq + f, to[0] * n_freq + to[1]))
        return lax.ppermute(x, ("chan", "freq"), pairs)

    def paired(at, count, off):
        to = ((at + off) ^ 1) - off
        return to if 0 <= to < count else at

    tail, head = strain[:, length - 2 * TBLK :], strain[:, : 2 * TBLK]
    even = lax.axis_index("freq") % 2 == 0
    ends = (jnp.where(even, tail, head), jnp.where(even, head, tail))
    other = moved(strain, lambda c, f: (c ^ 1, f))
    halos = [
        moved(ends[off], lambda c, f, o=off, k=flip: (c ^ k, paired(f, n_freq, o)))
        for off in range(2)
        for flip in range(2)
    ]

    quality_pad = jnp.pad(quality, (0, BAND + both))
    reach_pad = jnp.pad(offset_reach, (both, 0))
    quality_both = lax.dynamic_slice_in_dim(quality_pad, chip * both, both, 0)
    reach_pad = reach_pad.astype(jnp.float32)
    reach_own = lax.dynamic_slice_in_dim(reach_pad, (chip + 1) * both, both, 0)[None, :]
    reach_prev = lax.dynamic_slice_in_dim(reach_pad, chip * both, both, 0)[None, :]
    quality_ext = lax.dynamic_slice_in_dim(quality_pad, me * ch, ch + BAND, 0)
    count = pair_count(quality_ext, lax.dynamic_slice_in_dim(offset_reach, me * ch, ch, 0), BAND)

    half = rk // 2
    nb = block_bins(n_freq)
    steps = count_a * half // nb
    first = steps // 3
    chunks = (first, steps - first)
    parts = spectra(strain, other, halos, n_freq, chunks)
    usable = quality_both.astype(jnp.bfloat16)[None, :]
    blocks = []
    for k in range(len(chunks)):
        pieces = list(parts[k * n_freq : (k + 1) * n_freq])
        for d in range(1, n_freq):
            pieces[d] = moved(pieces[d], lambda c, f, d=d: (c, f ^ d))
        own = jnp.stack([x * usable for x in pieces])
        blocks.append(
            [own]
            + [
                moved(own, lambda c, f, o=off: (2 * paired(c // 2, n_chan // 2, o) + c % 2, f))
                for off in range(2)
            ]
        )
    results = []
    for k, (own, near_chip, off_chip) in enumerate(blocks):
        far_type = jnp.bfloat16 if k == len(blocks) - 1 else jnp.float32
        if k:
            own, results[-4], count = lax.optimization_barrier((own, results[-4], count))
        mine, theirs, far_mine, far_theirs = cross(
            own, near_chip, off_chip, reach_own, reach_prev, far_type
        )
        if k:
            tied = lax.optimization_barrier((theirs, far_mine, far_theirs, *results[-3:]))
            theirs, far_mine, far_theirs = tied[:3]
            results[-3:] = tied[3:]
        results += [
            mine,
            moved(theirs, lambda c, f: (c ^ 1, f)),
            moved(far_mine, lambda c, f: (c - 2, f)),
            moved(far_theirs, lambda c, f: ((c ^ 1) - 2, f)),
        ]
    return finish(count[None, :], results, count_a, half)[None]


def solution(mesh):
    return jax.shard_map(
        on_device,
        mesh=mesh,
        in_specs=(P("chan", "freq"), P(), P()),
        out_specs=P("chan", None, "freq", None),
        check_vma=False,
    )
```

```python
import functools
import math

import jax
import jax.numpy as jnp
import ml_dtypes
import numpy as np
from jax import lax
from jax.experimental import pallas as pl
from jax.experimental.pallas import tpu as pltpu
from jax.sharding import PartitionSpec as P

BAND = 256
TBLK = 128

band_low = 0.004
band_high = 0.48
level_eps = 1e-05
MIB = 1 << 20


def tap_values(offset, half_span):
    window = 0.5 + 0.5 * np.cos(np.pi * offset / (half_span + 1))
    response = 2.0 * band_high * np.sinc(2.0 * band_high * offset) - 2.0 * band_low * np.sinc(
        2.0 * band_low * offset
    )
    return np.where(np.abs(offset) <= half_span, window * response, 0.0)


def stencil_table(boxed):
    offset = np.arange(2 * TBLK)[None, :] + TBLK - np.arange(4 * TBLK)[:, None]
    if boxed:
        values = np.where(np.abs(offset) <= TBLK, 1.0, 0.0)
    else:
        values = tap_values(offset.astype(np.float64), TBLK)
    return values.astype(ml_dtypes.bfloat16)


def dft_tables(count_a, n_freq):
    pad_a = -(-count_a // 16) * 16
    length = count_a * TBLK
    index = np.arange(count_a)
    angle = (index[:, None] * index[None, :] % count_a) * (2.0 * np.pi / count_a)
    first = np.zeros((2, pad_a, pad_a))
    first[0, :count_a, :count_a] = np.cos(angle)
    first[1, :count_a, :count_a] = -np.sin(angle)
    first = first.reshape(2 * pad_a, pad_a).astype(ml_dtypes.bfloat16)
    twist = np.zeros((2, pad_a, TBLK), np.float32)
    turn = (index[:, None] * np.arange(TBLK)[None, :] % length) * (2.0 * np.pi / length)
    twist[0, :count_a] = np.cos(turn)
    twist[1, :count_a] = np.sin(turn)
    k2_count = TBLK // 2
    turn = (np.arange(k2_count)[:, None] * np.arange(TBLK)[None, :] % TBLK) * (2.0 * np.pi / TBLK)
    real = np.concatenate([np.cos(turn), np.sin(turn)], axis=1)
    imag = np.concatenate([-np.sin(turn), np.cos(turn)], axis=1)
    half = k2_count // n_freq // 2
    second = np.stack([real, imag]).reshape(2, n_freq, 2, half, 2 * TBLK)
    second = second.transpose(1, 2, 0, 3, 4).reshape(n_freq, 2, 2 * half, 2 * TBLK)
    return first, twist, second.astype(ml_dtypes.bfloat16)


def block_bins(n_freq):
    return 16 if n_freq <= 4 else 8


def whole(shape):
    return pl.BlockSpec(shape, lambda t: (0,) * len(shape))


def spectra_kernel(
    count_a,
    n_freq,
    chunks,
    own,
    other,
    near_own,
    near_other,
    off_own,
    off_other,
    taps,
    box,
    first,
    twist,
    second,
    *rest,
):
    outs = rest[: n_freq * len(chunks)]
    padded, filtered, magnitude, whitened, tw_re, tw_im = rest[len(outs) :]
    core, band = lax.axis_index("chan") % 2, lax.axis_index("freq")
    ch = own.shape[0]
    both = 2 * ch
    pad_a = first.shape[1]
    dot = functools.partial(jnp.dot, preferred_element_type=jnp.float32)

    even = band % 2 == 0
    sides = ((own, near_own, off_own), (other, near_other, off_other))
    for which, (mid, near, off) in enumerate(sides):
        near, off = near[...], off[...]
        lo, hi = jnp.where(even, off, near), jnp.where(even, near, off)
        lo = jnp.where(band > 0, lo, jnp.zeros_like(lo))
        hi = jnp.where(band < n_freq - 1, hi, jnp.zeros_like(hi))
        base = core if which == 0 else 1 - core
        rows = pl.ds(pl.multiple_of(base * ch, ch), ch)
        for j in range(2):
            padded[j, rows, :] = lo[:, j * TBLK : (j + 1) * TBLK]
            padded[count_a + 2 + j, rows, :] = hi[:, j * TBLK : (j + 1) * TBLK]
        for j in range(count_a):
            padded[2 + j, rows, :] = mid[:, j * TBLK : (j + 1) * TBLK]

    def fir(i, carry):
        j = 2 * i
        window = jnp.concatenate([padded[j + n] for n in range(4)], axis=1)
        result = dot(window, taps[...])
        for n in range(2):
            part = result[:, n * TBLK : (n + 1) * TBLK]
            filtered[j + n] = part
            magnitude[j + n] = jnp.abs(part).astype(jnp.bfloat16)
        return carry

    lax.fori_loop(0, count_a // 2 + 1, fir, 0, unroll=True)

    def whiten(i, carry):
        j = 2 * i
        window = jnp.concatenate([magnitude[j + n] for n in range(4)], axis=1)
        level = dot(window, box[...]) / (2 * TBLK + 1)
        for n in range(2):
            part = filtered[j + n + 1] / (level[:, n * TBLK : (n + 1) * TBLK] + level_eps)
            rows = pl.ds(pl.multiple_of((j + n) * both, both), both)
            whitened[rows, :] = part
        return carry

    lax.fori_loop(0, count_a // 2, whiten, 0, unroll=True)
    whitened[count_a * both : pad_a * both, :] = jnp.zeros(
        ((pad_a - count_a) * both, TBLK), jnp.float32
    )

    def sections(i, carry):
        c = 2 * i
        pair = [
            whitened[pl.ds(c + n, pad_a, stride=both), :].astype(jnp.bfloat16) for n in range(2)
        ]
        section = dot(first[...], jnp.concatenate(pair, axis=1))
        for n in range(2):
            re = section[:pad_a, n * TBLK : (n + 1) * TBLK]
            im = section[pad_a:, n * TBLK : (n + 1) * TBLK]
            rows = pl.ds(pl.multiple_of((c + n) * pad_a, pad_a), pad_a)
            tw_re[rows, :] = re * twist[0] + im * twist[1]
            tw_im[rows, :] = im * twist[0] - re * twist[1]
        return carry

    lax.fori_loop(0, both // 2, sections, 0, unroll=True)

    rk = second.shape[2]
    half = rk // 2
    group = block_bins(n_freq) // half
    scale = 1.0 / math.sqrt(count_a * TBLK)
    turn = jnp.concatenate([second[band ^ d, core] for d in range(n_freq)], axis=0)

    def bins(k, start, i):
        results = []
        for n in range(group):
            k1 = (start + i) * group + n
            re = tw_re[pl.ds(k1, both, stride=pad_a), :].astype(jnp.bfloat16)
            im = tw_im[pl.ds(k1, both, stride=pad_a), :].astype(jnp.bfloat16)
            result = lax.dot_general(
                turn,
                jnp.concatenate([re, im], axis=1),
                (((1,), (1,)), ((), ())),
                preferred_element_type=jnp.float32,
            )
            results.append(result * scale)
        rows = pl.ds(i * group * rk, group * rk)
        for d in range(n_freq):
            starts = [d * rk + p * half for p in range(2)]
            block = jnp.concatenate([r[s : s + half] for s in starts for r in results], axis=0)
            outs[k * n_freq + d][rows, :] = block.astype(jnp.bfloat16)

    start = 0
    for k, size in enumerate(chunks):
        for i in range(size):
            bins(k, start, i)
        start += size


def spectra(own, other, halos, n_freq, chunks):
    ch, length = own.shape
    count_a = length // TBLK
    first, twist, second = dft_tables(count_a, n_freq)
    rk = second.shape[2]
    pad_a = first.shape[1]
    both = 2 * ch
    rows = 2 * block_bins(n_freq)
    shapes = [(size * rows, both) for size in chunks for _ in range(n_freq)]
    tables = (stencil_table(False), stencil_table(True), first, twist, second)
    operands = (own, other, *halos, *(jnp.asarray(t) for t in tables))
    return pl.pallas_call(
        functools.partial(spectra_kernel, count_a, n_freq, chunks),
        grid=(1,),
        out_shape=[jax.ShapeDtypeStruct(shape, jnp.bfloat16) for shape in shapes],
        in_specs=[whole(x.shape) for x in operands],
        out_specs=[whole(shape) for shape in shapes],
        scratch_shapes=[
            pltpu.VMEM((count_a + 4, both, TBLK), jnp.bfloat16),
            pltpu.VMEM((count_a + 2, both, TBLK), jnp.float32),
            pltpu.VMEM((count_a + 2, both, TBLK), jnp.bfloat16),
            pltpu.VMEM((pad_a * both, TBLK), jnp.float32),
            pltpu.VMEM((both * pad_a, TBLK), jnp.float32),
            pltpu.VMEM((both * pad_a, TBLK), jnp.float32),
        ],
        compiler_params=pltpu.CompilerParams(vmem_limit_bytes=62 * MIB),
        cost_estimate=pl.CostEstimate(
            flops=6 * 10**9, bytes_accessed=4 * 10**6, transcendentals=0
        ),
        name="spectra",
    )(*operands)


def cross_kernel(
    per,
    reach_own,
    reach_prev,
    turn_ref,
    pick_ref,
    cut_ref,
    own_ref,
    near_chip_ref,
    off_chip_ref,
    mine_ref,
    theirs_ref,
    far_mine_ref,
    far_theirs_ref,
    w_near,
    w_far,
    edge,
    sum_one,
    sum_two,
    sum_far,
):
    step = pl.program_id(0)
    n_seg, rb, both = own_ref.shape
    rb //= per
    depth = turn_ref.shape[0]
    nb = pick_ref.shape[0]
    slabs = both // 8
    me = lax.axis_index("chan")
    first_core = me % 2 == 0
    chip = me // 2
    last_chip = lax.axis_size("chan") // 2 - 1

    def beside(j):
        rows = slice(j * rb, (j + 1) * rb)
        near, off = near_chip_ref[:, rows, :], off_chip_ref[:, rows, :]
        even = chip % 2 == 0
        prev, nxt = jnp.where(even, off, near), jnp.where(even, near, off)
        prev = jnp.where(chip > 0, prev, jnp.zeros_like(prev))
        nxt = jnp.where(chip < last_chip, nxt, jnp.zeros_like(nxt))
        return prev, nxt

    @pl.when(step == 0)
    def _():
        row = lax.broadcasted_iota(jnp.int32, (16, both), 0) % 8
        col = lax.broadcasted_iota(jnp.int32, (16, both), 1)
        offset = (both + col - row).astype(jnp.float32)
        columns = [
            jnp.broadcast_to(r[...], (both, both)).T for r in (reach_own, reach_prev)
        ]
        wide = jnp.concatenate([columns[1], columns[1]], axis=1)
        for a in range(slabs):
            mine = columns[0][a * 8 : a * 8 + 8]
            lent = columns[1][a * 8 : a * 8 + 8]
            mine = jnp.concatenate([mine, mine], axis=0)
            lent = jnp.concatenate([lent, lent], axis=0)
            inner = col < both - 8 * a
            w_near[a] = jnp.where(inner & ((col < row) | (offset < mine)), 1.0, 0.0)
            w_far[a] = jnp.where(~inner & (offset < lent), 1.0, 0.0)
        row = lax.broadcasted_iota(jnp.int32, (both, 2 * both), 0)
        col = lax.broadcasted_iota(jnp.int32, (both, 2 * both), 1)
        same = (row // (both // 2)) == (col // both)
        for d in range(1, 8):
            hit = same & (col % both == both - d) & (row % 8 >= d)
            hit = hit & (2 * both - d < wide)
            edge[(d - 1) * both : d * both, :] = jnp.where(hit, 1.0, 0.0).astype(jnp.bfloat16)

    def left_rows(block):
        re = block.astype(jnp.float32).T.astype(jnp.bfloat16)
        im = jnp.dot(re, turn_ref[...], preferred_element_type=jnp.float32)
        re = re.astype(jnp.float32).reshape(slabs, 8, depth)
        im = im.reshape(slabs, 8, depth)
        return jnp.stack([re, im], axis=1).reshape(slabs, 16, depth).astype(jnp.bfloat16)

    def dots(j):
        own = own_ref[:, j * rb : (j + 1) * rb, :].reshape(depth, both)
        prev, nxt = (x.reshape(depth, both) for x in beside(j))
        left = jnp.concatenate([left_rows(own), left_rows(prev)], axis=2)
        pick = pick_ref[...]

        zero = jnp.zeros_like(own)
        for a in range(slabs):
            g, first = divmod(a, slabs // 2)
            if a == 0:
                right = jnp.concatenate(
                    [jnp.concatenate([own, nxt], axis=1), jnp.concatenate([zero, zero], axis=1)],
                    axis=0,
                )
            else:
                moved_own = pltpu.roll(own, both - 8 * a, 1).reshape(depth // 16, 16, both)
                moved_next = pltpu.roll(nxt, both - 8 * a, 1).reshape(depth // 16, 16, both)
                cut = cut_ref[a][None]
                inner = moved_next * cut
                outer = moved_next - inner
                local = (moved_own * cut + outer).reshape(depth, both)
                inner = inner.reshape(depth, both)
                outer = outer.reshape(depth, both)
                right = jnp.concatenate(
                    [
                        jnp.concatenate([local, inner], axis=1),
                        jnp.concatenate([zero, outer], axis=1),
                    ],
                    axis=0,
                )
            rows = (left[a][None] * pick).reshape(nb * 16, 2 * depth)
            result = jnp.dot(rows, right, preferred_element_type=jnp.float32)
            one = result[:, :both]
            two = result[:, both:].reshape(nb, 16, both)
            near = (two * w_near[a][None]).reshape(nb * 16, both)
            far = (two * w_far[a][None]).reshape(nb * 16, both)
            if first == 0:
                sum_one[2 * j + g], sum_two[2 * j + g], sum_far[2 * j + g] = one, near, far
            else:
                sum_one[2 * j + g] += one
                sum_two[2 * j + g] += near
                sum_far[2 * j + g] += far


    def margins(j):
        def split(x):
            return x[:nb], x[nb:]

        prev, nxt = (x.astype(jnp.float32) for x in beside(j))
        lefts = [split(prev[s]) for s in range(n_seg)]
        rights = [split(nxt[s]) for s in range(n_seg)]
        pieces = []
        for d in range(1, 8):
            re = im = None
            for (xr, xi), (yr, yi) in zip(lefts, rights):
                yr, yi = pltpu.roll(yr, d, 1), pltpu.roll(yi, d, 1)
                r, i = xr * yr + xi * yi, xi * yr - xr * yi
                re, im = (r, i) if re is None else (re + r, im + i)
            pieces.append(jnp.concatenate([re, im], axis=0).astype(jnp.bfloat16))
        margin = jnp.dot(
            jnp.concatenate(pieces, axis=1), edge[...], preferred_element_type=jnp.float32
        )


        return margin

    def diag(j, margin):
        lane = lax.broadcasted_iota(jnp.int32, (nb, both), 1)
        for p in range(2):
            values = []
            for g in range(2):
                low = high = far = None
                for b in range(8):
                    rows = pl.ds(p * 8 + b, nb, stride=16)
                    one, two, three = sum_one[2 * j + g, rows, :], sum_two[2 * j + g, rows, :], sum_far[2 * j + g, rows, :]
                    if b == 0:
                        low, high, far = one, two, three
                        continue
                    low += pltpu.roll(jnp.where(lane >= b, one, two), both - b, 1)
                    high += pltpu.roll(jnp.where(lane >= b, two, 0.0), both - b, 1)
                    far += pltpu.roll(three, both - b, 1)
                far += margin[p * nb : (p + 1) * nb, g * both : (g + 1) * both]
                values.append((low, high, far))
            mine = [jnp.where(first_core, x, y) for x, y in zip(*values)]
            theirs = [jnp.where(first_core, y, x) for x, y in zip(*values)]
            for near_ref, far_ref, value in (
                (mine_ref, far_mine_ref, mine),
                (theirs_ref, far_theirs_ref, theirs),
            ):
                near_ref[p, j, :nb] = value[0]
                near_ref[p, j, nb:] = value[1]
                far_ref[p, j] = value[2].astype(far_ref.dtype)

    for j in range(per):
        dots(j)
    margin = [margins(j) for j in range(per)]
    for j in range(per):
        diag(j, margin[j])


def cross(own, near_chip, off_chip, reach_own, reach_prev, far_type):
    n_seg, rows, both = own.shape
    nb = block_bins(n_seg)
    rb = 2 * nb
    depth = n_seg * rb
    steps = rows // rb
    slabs = both // 8
    per = max(n for n in (1, 2, 4, 5) if steps % n == 0)
    lane = np.arange(depth)
    part = lane % rb // nb
    turn = np.zeros((depth, depth))
    turn[lane + np.where(part == 0, nb, -nb), lane] = np.where(part == 0, 1.0, -1.0)
    lane = np.arange(2 * depth)
    pick = (lane % nb == np.arange(nb)[:, None, None]).astype(np.float32)
    pick = np.broadcast_to(pick, (nb, 16, 2 * depth))
    cut = np.arange(both) < both - 8 * np.arange(slabs)[:, None, None]
    cut = np.broadcast_to(cut, (slabs, 16, both))
    tables = [jnp.asarray(x.astype(ml_dtypes.bfloat16)) for x in (turn, pick, cut)]
    fixed = (reach_own, reach_prev, *tables)
    near = jax.ShapeDtypeStruct((2, steps, 2 * nb, both), jnp.float32)
    far = jax.ShapeDtypeStruct((2, steps, nb, both), far_type)
    near_spec = pl.BlockSpec((2, per, 2 * nb, both), lambda t: (0, t, 0, 0))
    far_spec = pl.BlockSpec((2, per, nb, both), lambda t: (0, t, 0, 0))
    block = pl.BlockSpec((n_seg, per * rb, both), lambda t: (0, t, 0))
    return pl.pallas_call(
        functools.partial(cross_kernel, per),
        grid=(steps // per,),
        out_shape=[near, near, far, far],
        in_specs=[whole(x.shape) for x in fixed] + [block] * 3,
        out_specs=[near_spec, near_spec, far_spec, far_spec],
        scratch_shapes=[
            pltpu.VMEM((slabs, 16, both), jnp.float32),
            pltpu.VMEM((slabs, 16, both), jnp.float32),
            pltpu.VMEM((7 * both, 2 * both), jnp.bfloat16),
            pltpu.VMEM((2 * per, nb * 16, both), jnp.float32),
            pltpu.VMEM((2 * per, nb * 16, both), jnp.float32),
            pltpu.VMEM((2 * per, nb * 16, both), jnp.float32),
        ],
        compiler_params=pltpu.CompilerParams(
            dimension_semantics=("arbitrary",), vmem_limit_bytes=24 * MIB
        ),
        cost_estimate=pl.CostEstimate(
            flops=10**9 * steps, bytes_accessed=2 * 10**5 * steps, transcendentals=0
        ),
        name="cross",
    )(*fixed, own, near_chip, off_chip)


def finish_kernel(count_a, half, chunks, count, *rest):
    parts, out_ref, stage = rest[: 4 * chunks], rest[4 * chunks], rest[4 * chunks + 1]
    core = lax.axis_index("chan") % 2
    bins = out_ref.shape[1] // 2
    inverse = 1.0 / count[...]
    k1 = 0
    for chunk in range(chunks):
        mine, theirs, far_mine, far_theirs = parts[4 * chunk : 4 * chunk + 4]
        steps, nb, both = far_mine.shape[1:]
        for t in range(steps):
            for which, (near, far) in enumerate(((mine, far_mine), (theirs, far_theirs))):
                base = (core if which == 0 else 1 - core) * bins
                value = near[0, t]
                low = value[:nb] * inverse[:, :both]
                high = (value[nb:] + far[0, t].astype(jnp.float32)) * inverse[:, both:]
                for r, x in enumerate((low, high)):
                    for n in range(nb // half):
                        place = pl.ds(base + k1 + n, half, stride=count_a)
                        stage[r, place, :] = x[n * half : (n + 1) * half]
            k1 += nb // half
    for r in range(2):
        both = stage.shape[2]
        out_ref[0, :, r * both : (r + 1) * both] = stage[r]


def finish(count, parts, count_a, half):
    bins = count_a * half

    def half_of(shape):
        return pl.BlockSpec((1,) + shape[1:], lambda p: (p,) + (0,) * (len(shape) - 1))

    return pl.pallas_call(
        functools.partial(finish_kernel, count_a, half, len(parts) // 4),
        grid=(2,),
        out_shape=jax.ShapeDtypeStruct((2, 2 * bins, BAND), jnp.float32),
        in_specs=[whole(count.shape)] + [half_of(x.shape) for x in parts],
        out_specs=half_of((2, 2 * bins, BAND)),
        scratch_shapes=[pltpu.VMEM((2, 2 * bins, TBLK), jnp.float32)],
        compiler_params=pltpu.CompilerParams(vmem_limit_bytes=24 * MIB),
        name="finish",
    )(count, *parts)


def skew_rows(matrix, keep):
    height, width = matrix.shape
    flat = jnp.pad(matrix.reshape(height * width), (0, height))
    return flat.reshape(height, width + 1)[:, :keep]


def pair_count(quality_ext, reach_own, band):
    channel_count = reach_own.shape[0]
    ext_len = quality_ext.shape[0]
    partner = skew_rows(jnp.broadcast_to(quality_ext[None, :], (channel_count, ext_len)), band)
    offsets = jnp.arange(band, dtype=jnp.int32)[None, :]
    inside = (offsets < reach_own[:, None]).astype(jnp.int32)
    weight = quality_ext[:channel_count, None] * partner * inside
    return jnp.maximum(jnp.sum(weight.astype(jnp.float32), axis=0), 1.0)


def on_device(strain, quality, offset_reach):
    ch, length = strain.shape
    both = 2 * ch
    assert both == TBLK and BAND == 2 * both
    n_chan, n_freq = lax.axis_size("chan"), lax.axis_size("freq")
    count_a = length // TBLK
    rk = TBLK // 2 // n_freq
    me = lax.axis_index("chan")
    chip = me // 2

    def moved(x, target):
        pairs = []
        for c in range(n_chan):
            for f in range(n_freq):
                to = target(c, f)
                if 0 <= to[0] < n_chan and 0 <= to[1] < n_freq:
                    pairs.append((c * n_freq + f, to[0] * n_freq + to[1]))
        return lax.ppermute(x, ("chan", "freq"), pairs)

    def paired(at, count, off):
        to = ((at + off) ^ 1) - off
        return to if 0 <= to < count else at

    tail, head = strain[:, length - 2 * TBLK :], strain[:, : 2 * TBLK]
    even = lax.axis_index("freq") % 2 == 0
    ends = (jnp.where(even, tail, head), jnp.where(even, head, tail))
    other = moved(strain, lambda c, f: (c ^ 1, f))
    halos = [
        moved(ends[off], lambda c, f, o=off, k=flip: (c ^ k, paired(f, n_freq, o)))
        for off in range(2)
        for flip in range(2)
    ]

    quality_pad = jnp.pad(quality, (0, BAND + both))
    reach_pad = jnp.pad(offset_reach, (both, 0))
    quality_both = lax.dynamic_slice_in_dim(quality_pad, chip * both, both, 0)
    reach_pad = reach_pad.astype(jnp.float32)
    reach_own = lax.dynamic_slice_in_dim(reach_pad, (chip + 1) * both, both, 0)[None, :]
    reach_prev = lax.dynamic_slice_in_dim(reach_pad, chip * both, both, 0)[None, :]
    quality_ext = lax.dynamic_slice_in_dim(quality_pad, me * ch, ch + BAND, 0)
    count = pair_count(quality_ext, lax.dynamic_slice_in_dim(offset_reach, me * ch, ch, 0), BAND)

    half = rk // 2
    nb = block_bins(n_freq)
    steps = count_a * half // nb
    first = steps // 3
    chunks = (first, steps - first)
    parts = spectra(strain, other, halos, n_freq, chunks)
    usable = quality_both.astype(jnp.bfloat16)[None, :]
    blocks = []
    for k in range(len(chunks)):
        pieces = list(parts[k * n_freq : (k + 1) * n_freq])
        for d in range(1, n_freq):
            pieces[d] = moved(pieces[d], lambda c, f, d=d: (c, f ^ d))
        own = jnp.stack([x * usable for x in pieces])
        blocks.append(
            [own]
            + [
                moved(own, lambda c, f, o=off: (2 * paired(c // 2, n_chan // 2, o) + c % 2, f))
                for off in range(2)
            ]
        )
    results = []
    for k, (own, near_chip, off_chip) in enumerate(blocks):
        far_type = jnp.bfloat16 if k == len(blocks) - 1 else jnp.float32
        if k:
            own, results[-4], count = lax.optimization_barrier((own, results[-4], count))
        mine, theirs, far_mine, far_theirs = cross(
            own, near_chip, off_chip, reach_own, reach_prev, far_type
        )
        if k:
            tied = lax.optimization_barrier((theirs, far_mine, far_theirs, *results[-3:]))
            theirs, far_mine, far_theirs = tied[:3]
            results[-3:] = tied[3:]
        results += [
            mine,
            moved(theirs, lambda c, f: (c ^ 1, f)),
            moved(far_mine, lambda c, f: (c - 2, f)),
            moved(far_theirs, lambda c, f: ((c ^ 1) - 2, f)),
        ]
    return finish(count[None, :], results, count_a, half)[None]


def solution(mesh):
    return jax.shard_map(
        on_device,
        mesh=mesh,
        in_specs=(P("chan", "freq"), P(), P()),
        out_specs=P("chan", None, "freq", None),
        check_vma=False,
    )
```
